256 devices in a mesh: leaf: 32 (over z, y), front: 8 (over x, core).
Axes of the slice: x: 4, y: 4, z: 8, core: 2. Of those that a mesh axis runs over, the one named last changes fastest.
Arguments:
- front: float32 [40960, 8192], P('leaf', 'front'), may hold values from -2.5 to 515.06
- child_blocks: float32 [32, 32, 128, 1024], P('leaf', None, None, 'front'), may hold values from -0.1 to 0.25
- child_map: int32 [32, 32, 8], P('leaf', None, 'front'), may hold values from 0 to 79, as said below
- pattern: int32 [320, 64], P('leaf', 'front'), may hold values 0 or 1
Outputs:
- factored: float32 [40960, 8192], P('leaf', 'front')
The draws below stay inside these ranges and needn't reach their ends.
Inputs may be any that keep to these rules, and one draw needn't show every extreme that they name: `child_map`: for one receiving leaf index and one front index, the contribution blocks of the different senders name different blocks, and every block on the front's diagonal among the receiver's blocks is named by one of them.
All inputs are finite; a program needn't handle non-finite values. No bound on the sum of `pattern` on one device may be relied on, other than what follows from the above.
Results may differ from the reference program's by a relative error of at most 0.0003.
Values sent between devices are 32-bit elements; how exact they have to be, the bound alone decides.
A program may use at most 128 MiB of HBM per device.

```python
import jax
import jax.numpy as jnp
from jax import lax

B = 128
RB = 10
CB = 8
PANELS = 4
NBR = 320
NBC = 64
ROWS = 40960
COLS = 8192
N_LEAF = 32
N_FRONT = 8


def draw_front(key, part):
    key = jax.random.fold_in(key, 11)
    first = jax.random.fold_in(key, 0)
    third = jax.random.fold_in(key, 2)
    fourth = jax.random.fold_in(key, 3)
    row_pos = lax.broadcasted_iota(jnp.int32, (ROWS, COLS), 0)
    col_pos = lax.broadcasted_iota(jnp.int32, (ROWS, COLS), 1)
    leading_size = PANELS * B
    leading = (row_pos < leading_size) & (col_pos < leading_size)
    same_block = row_pos // B == col_pos // B
    limit = (B - 1) * 0.85 + (leading_size - B) * 0.75 + 0.25
    rough = jax.random.uniform(first, (ROWS, COLS), jnp.float32)
    stretch = jax.random.uniform(third, (ROWS, 1), jnp.float32)
    inner = -(0.2 + 0.4 * rough)
    outer = -(0.2 + 0.3 * rough)
    far_part = -0.5 + jnp.clip(0.6 * jax.random.normal(fourth, (ROWS, COLS), jnp.float32), -1.5, 1.5)
    lift = 1.05 + 0.25 * stretch
    values = jnp.where(leading, jnp.where(same_block, inner, outer), far_part)
    diagonal = jnp.where(row_pos < leading_size, limit * lift, 6.0 + far_part)
    return jnp.where(row_pos == col_pos, diagonal, values).astype(jnp.float32)


def draw_child_map(key, part):
    key = jax.random.fold_in(key, 7)
    first, second = jax.random.split(key, 2)
    slot_count = RB * CB
    slots = jnp.arange(slot_count, dtype=jnp.int32)[None, None, :]
    receivers = jnp.arange(N_LEAF, dtype=jnp.int32)[:, None, None]
    fronts = jnp.arange(N_FRONT, dtype=jnp.int32)[None, :, None]
    on_diagonal = (receivers * RB + slots // CB == fronts * CB + slots % CB).astype(jnp.int32)
    order_keys = jax.random.split(first, N_LEAF * N_FRONT)
    orders = jax.vmap(lambda single: jax.random.permutation(single, slot_count))(order_keys)
    orders = orders.reshape(N_LEAF, N_FRONT, slot_count).astype(jnp.int32)
    scores = orders + slot_count * on_diagonal
    ranked = jnp.argsort(-scores, axis=-1)
    chosen = ranked[..., :N_LEAF].astype(jnp.int32)
    shuffle_keys = jax.random.split(second, N_LEAF * N_FRONT)
    shuffles = jax.vmap(lambda single: jax.random.permutation(single, N_LEAF))(shuffle_keys)
    shuffles = shuffles.reshape(N_LEAF, N_FRONT, N_LEAF).astype(jnp.int32)
    picked = jnp.take_along_axis(chosen, shuffles, axis=-1)
    return picked.transpose(2, 0, 1).astype(jnp.int32)


def touch_ends(result, own_key, low, high):
    spot = [jax.random.randint(jax.random.fold_in(own_key, axis), (), 0, length) for axis, length in enumerate(result.shape)]
    widest = result.shape.index(max(result.shape))
    neighbour = spot[:widest] + [(spot[widest] + 1) % result.shape[widest]] + spot[widest + 1:]
    return result.at[tuple(spot)].set(low).at[tuple(neighbour)].set(high)


def block_scale(own_key, shape, pieces, least, largest):
    gain, own = 1.0, jax.random.fold_in(own_key, 6)
    for axis_at, parts in pieces:
        heights = jnp.exp(jax.random.uniform(jax.random.fold_in(own, axis_at), (parts,), jnp.float32, least / len(pieces), largest / len(pieces)))
        gain = gain * jnp.repeat(heights, shape[axis_at] // parts).reshape([-1 if axis == axis_at else 1 for axis in range(len(shape))])
    return gain


def setup_inputs(seed: int = 0) -> dict:
    streams_of = jax.random.split(jax.random.key(seed), 5)
    return {
        "front": draw_front(jax.random.fold_in(streams_of[4], 71), 0),
        "child_blocks": jnp.clip(-0.1 + 0.35 * jax.random.uniform(streams_of[1], (N_LEAF, N_LEAF, B, N_FRONT * B), jnp.float32) ** block_scale(streams_of[1], (N_LEAF, N_LEAF, B, N_FRONT * B), ((0, 32), (3, 8)), -0.2, 0.2), -0.1, 0.25),
        "child_map": draw_child_map(jax.random.fold_in(streams_of[4], 71), 0),
        "pattern": touch_ends((jax.random.randint(streams_of[3], (NBR, NBC), 0, 4) < 3).astype(jnp.int32), jax.random.fold_in(streams_of[3], 1), 0, 1),
    }


def reference(front, child_blocks, child_map, pattern):
    highest = lax.Precision.HIGHEST
    blocks = child_blocks.reshape(N_LEAF, N_LEAF, B, N_FRONT, B).transpose(0, 1, 3, 2, 4).reshape(-1, B, B)
    target_row = jnp.arange(N_LEAF, dtype=jnp.int32)[None, :, None] * RB + child_map // CB
    target_col = jnp.arange(N_FRONT, dtype=jnp.int32)[None, None, :] * CB + child_map % CB
    target = (target_row * NBC + target_col).reshape(-1).astype(jnp.int32)
    added = jax.ops.segment_sum(blocks, target, num_segments=NBR * NBC)
    added = added.reshape(NBR, NBC, B, B).transpose(0, 2, 1, 3).reshape(ROWS, COLS)
    row_index = jnp.arange(NBR, dtype=jnp.int32)[:, None]
    col_index = jnp.arange(NBC, dtype=jnp.int32)[None, :]
    keep = ((pattern == 1) | (row_index == col_index)) & (row_index >= col_index)
    matrix = jnp.where(keep[:, None, :, None], (front + added).reshape(NBR, B, NBC, B), 0.0).reshape(ROWS, COLS)
    row_block = jnp.arange(ROWS, dtype=jnp.int32) // B
    col_block = jnp.arange(COLS, dtype=jnp.int32) // B
    identity = jnp.eye(B, dtype=front.dtype)
    for panel in range(PANELS):
        start_at = panel * B
        pivot = matrix[start_at:start_at + B, start_at:start_at + B]
        symmetric = jnp.tril(pivot) + jnp.tril(pivot, -1).T
        factor = jnp.linalg.cholesky(symmetric)
        inverse = lax.linalg.triangular_solve(factor, identity, left_side=True, lower=True)
        column = matrix[:, start_at:start_at + B]
        solved = jnp.dot(column, inverse.T, precision=highest)
        lower = jnp.where(row_block[:, None] > panel, solved, 0.0)
        lower = jnp.concatenate([lower[:start_at], factor, lower[start_at + B:]], axis=0)
        across = lower[:COLS]

        def update_group(triple):
            rows_part, lower_part, blocks_part = triple
            product = jnp.dot(lower_part, across.T, precision=highest)
            active = (blocks_part[:, None] >= col_block[None, :]) & (col_block[None, :] > panel)
            return jnp.where(active, rows_part - product, rows_part)
        matrix = lax.map(update_group, (matrix.reshape(N_LEAF, RB * B, COLS), lower.reshape(N_LEAF, RB * B, B), row_block.reshape(N_LEAF, RB * B))).reshape(ROWS, COLS)
        matrix = jnp.concatenate([matrix[:, :start_at], lower, matrix[:, start_at + B:]], axis=1)
    return matrix
```

```python
import functools

import jax
import jax.numpy as jnp
from jax import lax
from jax.experimental import pallas as pl
from jax.experimental.pallas import tpu as pltpu
from jax.sharding import PartitionSpec as P

B = 128
RB = 10
CB = 8
PANELS = 4
W = PANELS * B
NL = 32
NF = 8
NY = 4
NZ = 8
PIECE = B // NY
NR = CB + PANELS
F32 = jnp.float32
BF16 = jnp.bfloat16
MESH = pl.DeviceIdType.MESH
HBM = pl.BlockSpec(memory_space=pl.ANY)
SMEM = pl.BlockSpec(memory_space=pltpu.SMEM)
VMEM = pl.BlockSpec(memory_space=pltpu.VMEM)


def exchange(
    child, maptile, front, pattern,
    arrived, code, rows, match,
    child_v, front_v, rows_v, map_v, code_v, code_s,
    a_send, a_recv, m_send, m_recv, x_send, x_recv, q_recv, qz_send, qy_send, qa_send, local,
):
    d = lax.axis_index("leaf")
    f = lax.axis_index("front")
    z, y = d // NY, d % NY
    x, core = f // 2, f % 2

    barrier = pltpu.get_barrier_semaphore()

    def greet_leaf(k, _):
        pl.semaphore_signal(
            barrier, inc=1, device_id=(lax.rem(d + k, NL), f), device_id_type=MESH
        )
        return 0

    def greet_front(k, _):
        pl.semaphore_signal(
            barrier, inc=1, device_id=(d, lax.rem(f + k, NF)), device_id_type=MESH
        )
        return 0

    lax.fori_loop(1, NL, greet_leaf, 0)
    lax.fori_loop(1, NF, greet_front, 0)
    pl.semaphore_wait(barrier, NL - 1 + NF - 1)

    def block_copy(k):
        to = lax.rem(d + k, NL)
        return pltpu.make_async_remote_copy(
            src_ref=child.at[to], dst_ref=arrived.at[d], send_sem=a_send.at[k],
            recv_sem=a_recv.at[k], device_id=(to, f), device_id_type=MESH,
        )

    def map_copy(k):
        to = lax.rem(d + k, NL)
        return pltpu.make_async_remote_copy(
            src_ref=maptile.at[to], dst_ref=map_v.at[d], send_sem=m_send.at[k],
            recv_sem=m_recv.at[k], device_id=(to, f), device_id_type=MESH,
        )

    def block_in(k):
        frm = lax.rem(d - k + NL, NL)
        return pltpu.make_async_remote_copy(
            src_ref=child.at[frm], dst_ref=arrived.at[frm], send_sem=a_send.at[k],
            recv_sem=a_recv.at[k], device_id=(frm, f), device_id_type=MESH,
        )

    def map_in(k):
        frm = lax.rem(d - k + NL, NL)
        return pltpu.make_async_remote_copy(
            src_ref=maptile.at[frm], dst_ref=map_v.at[frm], send_sem=m_send.at[k],
            recv_sem=m_recv.at[k], device_id=(frm, f), device_id_type=MESH,
        )

    own_block = pltpu.make_async_copy(child.at[d], arrived.at[d], local.at[0])
    own_map = pltpu.make_async_copy(maptile.at[d], map_v.at[d], local.at[1])

    def send_blocks():
        def step(k, _):
            map_copy(k).start()
            block_copy(k).start()
            return 0

        lax.fori_loop(1, NL, step, 0)

    def receive_blocks():
        def step(k, _):
            map_in(k).wait_recv()
            block_in(k).wait_recv()
            return 0

        lax.fori_loop(1, NL, step, 0)
        own_block.wait()
        own_map.wait()
        lane = lax.broadcasted_iota(jnp.int32, (8, B), 1)

        def latest(s, total):
            return jnp.maximum(total, jnp.where(map_v[s] == lane, s + 1, 0))

        code_v[...] = lax.fori_loop(0, NL, latest, jnp.zeros((8, B), jnp.int32))
        pltpu.make_async_copy(code_v, code, local.at[2]).start()
        pltpu.make_async_copy(code_v, code, local.at[2]).wait()

    own_block.start()
    own_map.start()

    @pl.when(f != 1)
    def _():
        send_blocks()

    def chain_copy(r, to):
        return pltpu.make_async_remote_copy(
            src_ref=rows.at[r], dst_ref=rows.at[r], send_sem=x_send.at[r, 0],
            recv_sem=x_recv.at[r], device_id=(d, to), device_id_type=MESH,
        )

    def pair_copy(r, to):
        return pltpu.make_async_remote_copy(
            src_ref=rows.at[r], dst_ref=rows.at[r], send_sem=x_send.at[r, 1],
            recv_sem=x_recv.at[r], device_id=(d, to), device_id_type=MESH,
        )

    def root_copy(r, to, way):
        return pltpu.make_async_remote_copy(
            src_ref=rows_v.at[r], dst_ref=rows.at[r], send_sem=x_send.at[r, way],
            recv_sem=x_recv.at[r], device_id=(d, to), device_id_type=MESH,
        )

    def root_next(r):
        return jnp.where(r % 2 == 0, 2, NF - 1)

    @pl.when(f == 0)
    def _():
        front_in = pltpu.make_async_copy(front.at[:, pl.ds(0, W)], front_v, local.at[3])
        front_in.start()
        receive_blocks()
        to_vmem = pltpu.make_async_copy(arrived, child_v, local.at[4])
        to_vmem.start()
        to_smem = pltpu.make_async_copy(code_v, code_s, local.at[5])
        to_smem.start()
        front_in.wait()
        to_smem.wait()
        to_vmem.wait()

        def form(r, _):
            r_glob = d * RB + r
            for c in range(PANELS):
                t = code_s[0, r * CB + c]
                block = child_v[jnp.maximum(t - 1, 0)]
                has = (t > 0).astype(F32)
                keep = ((pattern[r, c] == 1) | (r_glob == c)) & (r_glob >= c)
                raw = front_v[pl.ds(r * B, B), c * B : (c + 1) * B]
                rows_v[r, :, c * B : (c + 1) * B] = (raw + block * has) * keep.astype(F32)
            root_copy(r, root_next(r), 0).start()
            root_copy(r, 1, 1).start()
            pltpu.make_async_copy(rows_v.at[r], rows.at[r], local.at[6 + r]).start()
            return 0

        lax.fori_loop(0, RB, form, 0)

        def settle(r, _):
            pltpu.make_async_copy(rows_v.at[r], rows.at[r], local.at[6 + r]).wait()
            return 0

        lax.fori_loop(0, RB, settle, 0)

    pair = f + 1 - 2 * core
    onward = f + 2 - 4 * core
    has_onward = ((core == 0) & (x < 3)) | ((core == 1) & (x > 1))

    @pl.when(f != 0)
    def _():
        def step(r, _):
            pltpu.make_async_remote_copy(
                src_ref=rows.at[r], dst_ref=rows.at[r], send_sem=x_send.at[r, 0],
                recv_sem=x_recv.at[r], device_id=(d, 0), device_id_type=MESH,
            ).wait_recv()

            @pl.when((f >= 2) & (core == r % 2))
            def _():
                @pl.when(has_onward)
                def _():
                    chain_copy(r, onward).start()

                pair_copy(r, pair).start()

            return 0

        lax.fori_loop(0, RB, step, 0)

    @pl.when(f == 1)
    def _():
        send_blocks()

    def where_from(i):
        r = jnp.where(i < CB, f * CB + i, i - CB)
        source = r // RB
        zs, ys = source // NY, source % NY
        return r % RB, ys, lax.rem(z - zs + NZ, NZ)

    def piece_of(ref, i, q):
        return ref.at[i, pl.ds(pl.multiple_of(q * PIECE, PIECE), PIECE)]

    def piece_copy(src, i, q, to_z, to_y, sem):
        return pltpu.make_async_remote_copy(
            src_ref=src, dst_ref=piece_of(match, i, q), send_sem=sem,
            recv_sem=q_recv.at[i, q], device_id=(to_z * NY + to_y, f), device_id_type=MESH,
        )

    def z_copy(src, i, up):
        to = lax.rem(z + (1 if up else NZ - 1), NZ)
        return piece_copy(src, i, y, to, y, qz_send.at[i, 0 if up else 1])

    def match_row(i, act):
        r_loc, ys, zr = where_from(i)
        at_source = (zr == 0) & (y == ys)

        @pl.when(at_source)
        def _():
            whole = pltpu.make_async_copy(rows.at[r_loc], match.at[i], local.at[16 + i])
            mine = piece_of(rows, r_loc, y)
            act(z_copy(mine, i, True))
            act(z_copy(mine, i, False))
            for k in range(1, NY):
                q = lax.rem(y + k, NY)
                act(piece_copy(piece_of(rows, r_loc, q), i, q, z, q, qa_send.at[i, k]))
            for k in range(1, NY):
                q = lax.rem(y + k, NY)
                act(piece_copy(mine, i, y, z, q, qy_send.at[i, k]))
            act(whole, here=True)

        @pl.when(jnp.logical_not(at_source))
        def _():
            mine = piece_of(match, i, y)
            act(None, i, y)

            @pl.when(zr < NZ // 2)
            def _():
                act(z_copy(mine, i, True))

            @pl.when((zr == 0) | (zr > NZ // 2 + 1))
            def _():
                act(z_copy(mine, i, False))

            for k in range(1, NY):
                q = lax.rem(y + k, NY)

                @pl.when((zr != 0) | (q != ys))
                def _():
                    act(piece_copy(mine, i, y, z, q, qy_send.at[i, k]))

                act(None, i, q, late=True)

    def piece_in(i, q):
        piece_copy(piece_of(match, i, q), i, q, z, lax.rem(y + 1, NY), qy_send.at[i, 1]).wait_recv()

    def begin(copy, i=None, q=None, late=False, here=False):
        if copy is not None:
            copy.start()
        elif not late:
            piece_in(i, q)

    def finish(copy, i=None, q=None, late=False, here=False):
        if copy is None:
            if late:
                piece_in(i, q)
        elif here:
            copy.wait()
        else:
            copy.wait_send()

    def run(act):
        def step(n, _):
            match_row(lax.rem(n + CB, NR), act)
            return 0

        lax.fori_loop(0, NR, step, 0)

    run(begin)

    @pl.when(f != 0)
    def _():
        receive_blocks()

    run(finish)

    def sent(k, _):
        map_copy(k).wait_send()
        block_copy(k).wait_send()
        return 0

    lax.fori_loop(1, NL, sent, 0)

    def row_sent(r, _):
        @pl.when(f == 0)
        def _():
            root_copy(r, root_next(r), 0).wait_send()
            root_copy(r, 1, 1).wait_send()

        @pl.when((f >= 2) & (core == r % 2))
        def _():
            @pl.when(has_onward)
            def _():
                chain_copy(r, onward).wait_send()

            pair_copy(r, pair).wait_send()

        return 0

    lax.fori_loop(0, RB, row_sent, 0)


def exchange_call(child, maptile, front, pattern):
    dma = pltpu.SemaphoreType.DMA
    shape = jax.ShapeDtypeStruct
    return pl.pallas_call(
        exchange,
        out_shape=(
            shape((NL, B, B), F32), shape((8, B), jnp.int32),
            shape((RB, B, W), F32), shape((NR, B, W), F32),
        ),
        in_specs=[HBM, HBM, HBM, SMEM],
        out_specs=(HBM,) * 4,
        scratch_shapes=[
            pltpu.VMEM((NL, B, B), F32), pltpu.VMEM((RB * B, W), F32),
            pltpu.VMEM((RB, B, W), F32), pltpu.VMEM((NL, 8, B), jnp.int32),
            pltpu.VMEM((8, B), jnp.int32), pltpu.SMEM((8, B), jnp.int32),
            dma((NL,)), dma((NL,)), dma((NL,)), dma((NL,)), dma((RB, 2)), dma((RB,)),
            dma((NR, NY)), dma((NR, 2)), dma((NR, NY)), dma((NR, NY)), dma((16 + NR,)),
        ],
        compiler_params=pltpu.CompilerParams(
            collective_id=0, has_side_effects=True, vmem_limit_bytes=32 << 20
        ),
    )(child, maptile, front, pattern)


def factor_block(s):
    sub = lax.broadcasted_iota(jnp.int32, (8, B), 0)
    lane = lax.broadcasted_iota(jnp.int32, (8, B), 1)
    groups = B // 8

    def down(value, i):
        return jnp.broadcast_to(value[i : i + 1, :], (8, B))

    left = [s[8 * g : 8 * g + 8, :] for g in range(groups)]
    right = [(lane == sub + 8 * g).astype(F32) for g in range(groups)]
    upper, inverse = [], []
    for p in range(groups):
        cols = [
            [jnp.broadcast_to(left[g][:, 8 * p + i : 8 * p + i + 1], (8, B)) for g in range(p, groups)]
            for i in range(8)
        ]
        done_l = jnp.zeros((8, B), F32)
        done_r = jnp.zeros((8, B), F32)
        for i in range(8):
            scale = lax.rsqrt(down(cols[i][0], i))
            col = [value * scale for value in cols[i]]
            row_l = down(left[p], i) * scale
            row_r = down(right[p], i) * scale
            done_l = jnp.where(sub == i, row_l, done_l)
            done_r = jnp.where(sub == i, row_r, done_r)
            for k in range(i + 1, 8):
                at = down(col[0], k)
                cols[k] = [v - w * at for v, w in zip(cols[k], col)]
            for g in range(p, groups):
                left[g] = left[g] - col[g - p] * row_l
                right[g] = right[g] - col[g - p] * row_r
        upper.append(jnp.where(lane >= sub + 8 * p, done_l, 0.0))
        inverse.append(done_r)
    return jnp.concatenate(upper, 0), jnp.concatenate(inverse, 0)


def dot_exact(a, b, contract):
    return lax.dot_general(
        a, b, (contract, ((), ())), precision=lax.Precision.HIGHEST, preferred_element_type=F32
    )


NT = ((1,), (1,))
NN = ((1,), (0,))


def factor_lead(work, pivots, inv):
    r = lax.broadcasted_iota(jnp.int32, (B, B), 0)
    c = lax.broadcasted_iota(jnp.int32, (B, B), 1)
    inv[...] = jnp.zeros_like(inv)
    for k in range(PANELS):
        at = slice(B * k, B * k + B)
        pivot = work[at, at]
        upper, inverse = factor_block(jnp.where(r >= c, pivot, pivot.T))
        pivots[k] = upper.T
        inv[at, at] = inverse
        if k < PANELS - 1:
            below = slice(B * k + B, W)
            lower = dot_exact(work[below, at], inverse, NT)
            work[below, at] = lower
            work[below, below] = work[below, below] - dot_exact(lower, lower, NT)
    for k in range(1, PANELS):
        at, before = slice(B * k, B * k + B), slice(0, B * k)
        inv[at, before] = -dot_exact(inv[at, at], dot_exact(work[at, before], inv[before, before], NN), NN)


def halves(a):
    high = a.astype(BF16)
    return high, (a - high.astype(F32)).astype(BF16)


def dot_split(a, b):
    (ah, al), (bh, bl) = a, b
    dot = functools.partial(
        lax.dot_general, dimension_numbers=(NT, ((), ())), preferred_element_type=F32
    )
    return dot(ah, bh) + (dot(al, bh) + dot(ah, bl))


STEP = 2


def finish_kernel(
    code, pattern, front, rows, match, arrived, out,
    work, pivots, inv, inv_h, inv_l, across_h, across_l,
):
    n = pl.program_id(0)
    d = lax.axis_index("leaf")
    f = lax.axis_index("front")

    @pl.when(n == 0)
    def _():
        for k in range(PANELS):
            work[B * k : B * k + B, :] = match[CB + k]
        factor_lead(work, pivots, inv)
        inv_h[...], inv_l[...] = halves(inv[...])
        for i in range(0, CB, STEP):
            part = match[i : i + STEP].reshape(STEP * B, W)
            lower = dot_split(halves(part), (inv_h[...], inv_l[...]))
            at = slice(i * B, (i + STEP) * B)
            across_h[at, :], across_l[at, :] = halves(lower)

    lower = dot_split(halves(rows[...].reshape(STEP * B, W)), (inv_h[...], inv_l[...]))
    product = dot_split(halves(lower), (across_h[...], across_l[...]))
    for rr in range(STEP):
        r = n * STEP + rr
        r_glob = d * RB + r
        rs = slice(rr * B, rr * B + B)
        for c in range(CB):
            c_glob = f * CB + c
            cs = slice(c * B, c * B + B)
            t = code[0, r * CB + c]
            keep = ((pattern[r, c] == 1) | (r_glob == c_glob)) & (r_glob >= c_glob)
            active = (r_glob >= c_glob) & (c_glob >= PANELS)
            block = arrived[jnp.maximum(t - 1, 0)]
            value = (front[rs, cs] + block * (t > 0).astype(F32)) * keep.astype(F32)
            out[rs, cs] = value - product[rs, cs] * active.astype(F32)

        @pl.when(f == 0)
        def _():
            for c in range(PANELS):
                cs = slice(c * B, c * B + B)
                solved = lower[rs, cs] * (r_glob > c).astype(F32)
                out[rs, cs] = solved + pivots[c] * (r_glob == c).astype(F32)


def finish_call(code, pattern, front, rows, match, arrived):
    whole = lambda *shape: pl.BlockSpec(shape, lambda n, *_: (0,) * len(shape))
    return pl.pallas_call(
        finish_kernel,
        out_shape=jax.ShapeDtypeStruct(front.shape, F32),
        grid_spec=pltpu.PrefetchScalarGridSpec(
            num_scalar_prefetch=2,
            grid=(RB // STEP,),
            in_specs=[
                pl.BlockSpec((STEP * B, CB * B), lambda n, *_: (n, 0)),
                pl.BlockSpec((STEP, B, W), lambda n, *_: (n, 0, 0)),
                whole(NR, B, W),
                whole(NL, B, B),
            ],
            out_specs=pl.BlockSpec((STEP * B, CB * B), lambda n, *_: (n, 0)),
            scratch_shapes=[
                pltpu.VMEM((W, W), F32), pltpu.VMEM((PANELS, B, B), F32), pltpu.VMEM((W, W), F32),
                pltpu.VMEM((W, W), BF16), pltpu.VMEM((W, W), BF16),
                pltpu.VMEM((CB * B, W), BF16), pltpu.VMEM((CB * B, W), BF16),
            ],
        ),
        compiler_params=pltpu.CompilerParams(vmem_limit_bytes=56 << 20),
    )(code, pattern, front, rows, match, arrived)


def body(front, child_blocks, child_map, pattern):
    child = child_blocks.reshape(NL, B, B)
    maptile = jnp.broadcast_to(child_map.reshape(NL, 1, 1), (NL, 8, B))
    arrived, code, rows, match = exchange_call(child, maptile, front, pattern)
    return finish_call(code, pattern, front, rows, match, arrived)


def solution(mesh):
    placed = (
        P("leaf", "front"),
        P("leaf", None, None, "front"),
        P("leaf", None, "front"),
        P("leaf", "front"),
    )
    return jax.shard_map(
        body, mesh=mesh, in_specs=placed, out_specs=P("leaf", "front"), check_vma=False
    )
```

```python
import functools

import jax
import jax.numpy as jnp
from jax import lax
from jax.experimental import pallas as pl
from jax.experimental.pallas import tpu as pltpu
from jax.sharding import PartitionSpec as P

B = 128
RB = 10
CB = 8
PANELS = 4
W = PANELS * B
NL = 32
NF = 8
NY = 4
NZ = 8
PIECE = B // NY
LR = 3
NR = CB + LR
CHUNK = B // 2
NC = RB * B // CHUNK
F32 = jnp.float32
BF16 = jnp.bfloat16
MESH = pl.DeviceIdType.MESH
HBM = pl.BlockSpec(memory_space=pl.ANY)
SMEM = pl.BlockSpec(memory_space=pltpu.SMEM)
VMEM = pl.BlockSpec(memory_space=pltpu.VMEM)


def exchange(
    child, maptile, front, pattern,
    arrived_out, code, rows_out, match_out, pivots_out,
    child_v, arrived, front_v, rows, match, work, inv, pivots, map_v, code_v, code_s,
    a_send, a_recv, m_send, m_recv, x_send, x_recv, l_send, l_recv, t_send, t_recv,
    q_recv, qz_send, qy_send, qa_send, local,
):
    d = lax.axis_index("leaf")
    f = lax.axis_index("front")
    z, y = d // NY, d % NY
    x, core = f // 2, f % 2

    child_in = pltpu.make_async_copy(child, child_v, local.at[4])
    child_in.start()
    front_in = pltpu.make_async_copy(front.at[:, pl.ds(0, W)], front_v, local.at[3])

    @pl.when(f == 0)
    def _():
        front_in.start()

    barrier = pltpu.get_barrier_semaphore()

    def greet_leaf(k, _):
        pl.semaphore_signal(
            barrier, inc=1, device_id=(lax.rem(d + k, NL), f), device_id_type=MESH
        )
        return 0

    def greet_front(k, _):
        pl.semaphore_signal(
            barrier, inc=1, device_id=(d, lax.rem(f + k, NF)), device_id_type=MESH
        )
        return 0

    lax.fori_loop(1, NL, greet_leaf, 0)
    lax.fori_loop(1, NF, greet_front, 0)
    pl.semaphore_wait(barrier, NL - 1 + NF - 1)

    child_in.wait()

    def block_copy(k):
        to = lax.rem(d + k, NL)
        return pltpu.make_async_remote_copy(
            src_ref=child_v.at[to], dst_ref=arrived.at[d], send_sem=a_send.at[k],
            recv_sem=a_recv.at[k], device_id=(to, f), device_id_type=MESH,
        )

    def map_copy(k):
        to = lax.rem(d + k, NL)
        return pltpu.make_async_remote_copy(
            src_ref=maptile.at[to], dst_ref=map_v.at[d], send_sem=m_send.at[k],
            recv_sem=m_recv.at[k], device_id=(to, f), device_id_type=MESH,
        )

    def block_in(k):
        frm = lax.rem(d - k + NL, NL)
        return pltpu.make_async_remote_copy(
            src_ref=child_v.at[frm], dst_ref=arrived.at[frm], send_sem=a_send.at[k],
            recv_sem=a_recv.at[k], device_id=(frm, f), device_id_type=MESH,
        )

    def map_in(k):
        frm = lax.rem(d - k + NL, NL)
        return pltpu.make_async_remote_copy(
            src_ref=maptile.at[frm], dst_ref=map_v.at[frm], send_sem=m_send.at[k],
            recv_sem=m_recv.at[k], device_id=(frm, f), device_id_type=MESH,
        )

    own_block = pltpu.make_async_copy(child_v.at[d], arrived.at[d], local.at[0])
    own_map = pltpu.make_async_copy(maptile.at[d], map_v.at[d], local.at[1])

    def send_blocks():
        def step(k, _):
            map_copy(k).start()
            block_copy(k).start()
            return 0

        lax.fori_loop(1, NL, step, 0)

    def receive_blocks():
        def step(k, _):
            map_in(k).wait_recv()
            block_in(k).wait_recv()
            return 0

        lax.fori_loop(1, NL, step, 0)
        own_block.wait()
        own_map.wait()
        lane = lax.broadcasted_iota(jnp.int32, (8, B), 1)

        def latest(s, total):
            return jnp.maximum(total, jnp.where(map_v[s] == lane, s + 1, 0))

        code_v[...] = lax.fori_loop(0, NL, latest, jnp.zeros((8, B), jnp.int32))
        pltpu.make_async_copy(code_v, code, local.at[2]).start()
        pltpu.make_async_copy(arrived, arrived_out, local.at[0]).start()

    own_block.start()
    own_map.start()

    @pl.when(f != 1)
    def _():
        send_blocks()

    def chunk_of(j):
        return rows.at[pl.ds(pl.multiple_of(j * CHUNK, CHUNK), CHUNK)]

    def chunk_copy(j, to, way):
        return pltpu.make_async_remote_copy(
            src_ref=chunk_of(j), dst_ref=chunk_of(j), send_sem=x_send.at[j, way],
            recv_sem=x_recv.at[j], device_id=(d, to), device_id_type=MESH,
        )

    def root_next(j):
        return jnp.where(j % 2 == 0, 2, NF - 1)

    @pl.when(f == 0)
    def _():
        receive_blocks()
        to_smem = pltpu.make_async_copy(code_v, code_s, local.at[3])
        front_in.wait()
        to_smem.start()
        to_smem.wait()

        def form(r, _):
            r_glob = d * RB + r
            at = pl.ds(pl.multiple_of(r * B, B), B)
            for c in range(PANELS):
                t = code_s[0, r * CB + c]
                block = arrived[jnp.maximum(t - 1, 0)]
                has = (t > 0).astype(F32)
                keep = ((pattern[r, c] == 1) | (r_glob == c)) & (r_glob >= c)
                raw = front_v[at, c * B : (c + 1) * B]
                rows[at, c * B : (c + 1) * B] = (raw + block * has) * keep.astype(F32)
            for h in range(2):
                j = 2 * r + h
                chunk_copy(j, root_next(j), 0).start()
                chunk_copy(j, 1, 1).start()
            return 0

        lax.fori_loop(0, RB, form, 0)

    pair = f + 1 - 2 * core
    onward = f + 2 - 4 * core
    has_onward = ((core == 0) & (x < 3)) | ((core == 1) & (x > 1))

    @pl.when(f != 0)
    def _():
        def passing(n, _):
            j = 2 * n + core
            chunk_copy(j, 0, 0).wait_recv()

            @pl.when(f >= 2)
            def _():
                @pl.when(has_onward)
                def _():
                    chunk_copy(j, onward, 0).start()

                chunk_copy(j, pair, 1).start()

            return 0

        def ending(n, _):
            chunk_copy(2 * n + 1 - core, 0, 0).wait_recv()
            return 0

        lax.fori_loop(0, NC // 2, passing, 0)
        lax.fori_loop(0, NC // 2, ending, 0)

    @pl.when(f == 1)
    def _():
        send_blocks()

    def where_from(i, lead):
        r = 0 if lead else f * CB + i
        source = r // RB
        zs, ys = source // NY, source % NY
        return r % RB, ys, lax.rem(z - zs + NZ, NZ)

    def row_of(ref, i):
        return ref.at[pl.ds(pl.multiple_of(i * B, B), B)]

    def piece_of(ref, i, q):
        return ref.at[pl.ds(pl.multiple_of(i * B + q * PIECE, PIECE), PIECE)]

    def piece_copy(src, i, q, to_z, to_y, sem):
        return pltpu.make_async_remote_copy(
            src_ref=src, dst_ref=piece_of(match, i, q), send_sem=sem,
            recv_sem=q_recv.at[i, q], device_id=(to_z * NY + to_y, f), device_id_type=MESH,
        )

    def z_copy(src, i, up):
        to = lax.rem(z + (1 if up else NZ - 1), NZ)
        return piece_copy(src, i, y, to, y, qz_send.at[i, 0 if up else 1])

    def match_row(i, act, lead):
        r_loc, ys, zr = where_from(i, lead)
        held, r_at = (match, i) if lead else (rows, r_loc)
        at_source = (zr == 0) & (y == ys)

        @pl.when(at_source)
        def _():
            mine = piece_of(held, r_at, y)
            act(z_copy(mine, i, True))
            act(z_copy(mine, i, False))
            for k in range(1, NY):
                q = lax.rem(y + k, NY)
                act(piece_copy(piece_of(held, r_at, q), i, q, z, q, qa_send.at[i, k]))
            for k in range(1, NY):
                q = lax.rem(y + k, NY)
                act(piece_copy(mine, i, y, z, q, qy_send.at[i, k]))
            if not lead:
                act(
                    pltpu.make_async_copy(row_of(rows, r_loc), row_of(match, i), local.at[16 + i]),
                    here=True,
                )

        @pl.when(jnp.logical_not(at_source))
        def _():
            mine = piece_of(match, i, y)
            act(None, i, y)

            @pl.when(zr < NZ // 2)
            def _():
                act(z_copy(mine, i, True))

            @pl.when((zr == 0) | (zr > NZ // 2 + 1))
            def _():
                act(z_copy(mine, i, False))

            for k in range(1, NY):
                q = lax.rem(y + k, NY)

                @pl.when((zr != 0) | (q != ys))
                def _():
                    act(piece_copy(mine, i, y, z, q, qy_send.at[i, k]))

                act(None, i, q, late=True)

    def piece_in(i, q):
        piece_copy(piece_of(match, i, q), i, q, z, lax.rem(y + 1, NY), qy_send.at[i, 1]).wait_recv()

    def begin(copy, i=None, q=None, late=False, here=False):
        if copy is not None:
            copy.start()
        elif not late:
            piece_in(i, q)

    def finish(copy, i=None, q=None, late=False, here=False):
        if copy is None:
            if late:
                piece_in(i, q)
        elif here:
            copy.wait()
        else:
            copy.wait_send()

    def run(act, first, last, lead):
        def step(i, _):
            match_row(i, act, lead)
            return 0

        lax.fori_loop(first, last, step, 0)

    def lead_copy(i, to, way):
        return pltpu.make_async_remote_copy(
            src_ref=row_of(match, i), dst_ref=row_of(match, i), send_sem=l_send.at[i - CB, way],
            recv_sem=l_recv.at[i - CB], device_id=(d, to), device_id_type=MESH,
        )

    def twin_copy(i, to):
        return pltpu.make_async_remote_copy(
            src_ref=row_of(match, i), dst_ref=row_of(match, i), send_sem=t_send.at[i - CB],
            recv_sem=t_recv.at[i - CB], device_id=(d, to), device_id_type=MESH,
        )

    keep_rows = pltpu.make_async_copy(rows, rows_out, local.at[7])
    keep_rows.start()
    run(begin, 0, CB, False)
    is_root = (d == 0) & (f == 0)
    keep_pivots = pltpu.make_async_copy(pivots, pivots_out, local.at[6])

    @pl.when(is_root)
    def _():
        work[...] = rows[0:W, :]
        factor_lead(work, pivots, inv)
        keep_pivots.start()
        match[CB * B :, :] = jnp.zeros((LR * B, W), F32)
        for i in range(PANELS):
            for j in range(i + 1):
                n = i * (i + 1) // 2 + j
                at = (CB + n // PANELS) * B
                to = n % PANELS * B
                match[at : at + B, to : to + B] = inv[i * B : i * B + B, j * B : j * B + B]
        for i in range(CB, NR):
            lead_copy(i, 2, 0).start()
            lead_copy(i, NF - 2, 1).start()

    @pl.when((d == 0) & (core == 0) & (f != 0))
    def _():
        for i in range(CB, NR):
            lead_copy(i, 0, 0).wait_recv()

            @pl.when(f == 2)
            def _():
                lead_copy(i, 4, 0).start()

    @pl.when(core == 0)
    def _():
        run(begin, CB, NR, True)

    @pl.when(f != 0)
    def _():
        receive_blocks()

    run(finish, 0, CB, False)

    @pl.when(core == 0)
    def _():
        run(finish, CB, NR, True)
        for i in range(CB, NR):
            twin_copy(i, f + 1).start()
        for i in range(CB, NR):
            twin_copy(i, f + 1).wait_send()

    @pl.when(core == 1)
    def _():
        for i in range(CB, NR):
            twin_copy(i, f - 1).wait_recv()

    keep_match = pltpu.make_async_copy(match, match_out, local.at[5])
    keep_match.start()

    @pl.when(is_root)
    def _():
        for i in range(CB, NR):
            lead_copy(i, 2, 0).wait_send()
            lead_copy(i, NF - 2, 1).wait_send()
        keep_pivots.wait()

    @pl.when((d == 0) & (f == 2))
    def _():
        for i in range(CB, NR):
            lead_copy(i, 4, 0).wait_send()

    def sent(k, _):
        map_copy(k).wait_send()
        block_copy(k).wait_send()
        return 0

    lax.fori_loop(1, NL, sent, 0)

    @pl.when(f == 0)
    def _():
        def chunk_sent(j, _):
            chunk_copy(j, root_next(j), 0).wait_send()
            chunk_copy(j, 1, 1).wait_send()
            return 0

        lax.fori_loop(0, NC, chunk_sent, 0)

    @pl.when(f >= 2)
    def _():
        def chunk_sent(n, _):
            j = 2 * n + core

            @pl.when(has_onward)
            def _():
                chunk_copy(j, onward, 0).wait_send()

            chunk_copy(j, pair, 1).wait_send()
            return 0

        lax.fori_loop(0, NC // 2, chunk_sent, 0)

    keep_rows.wait()
    keep_match.wait()
    pltpu.make_async_copy(code_v, code, local.at[2]).wait()
    pltpu.make_async_copy(arrived, arrived_out, local.at[0]).wait()


def exchange_call(child, maptile, front, pattern):
    dma = pltpu.SemaphoreType.DMA
    shape = jax.ShapeDtypeStruct
    return pl.pallas_call(
        exchange,
        out_shape=(
            shape((NL, B, B), F32), shape((8, B), jnp.int32),
            shape((RB * B, W), F32), shape((NR * B, W), F32), shape((PANELS, B, B), F32),
        ),
        in_specs=[HBM, HBM, HBM, SMEM],
        out_specs=(HBM,) * 5,
        scratch_shapes=[
            pltpu.VMEM((NL, B, B), F32), pltpu.VMEM((NL, B, B), F32),
            pltpu.VMEM((RB * B, W), F32), pltpu.VMEM((RB * B, W), F32),
            pltpu.VMEM((NR * B, W), F32), pltpu.VMEM((W, W), F32), pltpu.VMEM((W, W), F32),
            pltpu.VMEM((PANELS, B, B), F32), pltpu.VMEM((NL, 8, B), jnp.int32),
            pltpu.VMEM((8, B), jnp.int32), pltpu.SMEM((8, B), jnp.int32),
            dma((NL,)), dma((NL,)), dma((NL,)), dma((NL,)), dma((NC, 2)), dma((NC,)),
            dma((LR, 2)), dma((LR,)), dma((LR,)), dma((LR,)),
            dma((NR, NY)), dma((NR, 2)), dma((NR, NY)), dma((NR, NY)), dma((16 + NR,)),
        ],
        compiler_params=pltpu.CompilerParams(
            collective_id=0, has_side_effects=True, vmem_limit_bytes=56 << 20
        ),
    )(child, maptile, front, pattern)


def factor_block(s):
    sub = lax.broadcasted_iota(jnp.int32, (8, B), 0)
    lane = lax.broadcasted_iota(jnp.int32, (8, B), 1)
    groups = B // 8

    def down(value, i):
        return jnp.broadcast_to(value[i : i + 1, :], (8, B))

    left = [s[8 * g : 8 * g + 8, :] for g in range(groups)]
    right = [(lane == sub + 8 * g).astype(F32) for g in range(groups)]
    upper, inverse = [], []
    for p in range(groups):
        cols = [
            [jnp.broadcast_to(left[g][:, 8 * p + i : 8 * p + i + 1], (8, B)) for g in range(p, groups)]
            for i in range(8)
        ]
        done_l = jnp.zeros((8, B), F32)
        done_r = jnp.zeros((8, B), F32)
        for i in range(8):
            scale = lax.rsqrt(down(cols[i][0], i))
            col = [value * scale for value in cols[i]]
            row_l = down(left[p], i) * scale
            row_r = down(right[p], i) * scale
            done_l = jnp.where(sub == i, row_l, done_l)
            done_r = jnp.where(sub == i, row_r, done_r)
            for k in range(i + 1, 8):
                at = down(col[0], k)
                cols[k] = [v - w * at for v, w in zip(cols[k], col)]
            for g in range(p, groups):
                left[g] = left[g] - col[g - p] * row_l
                right[g] = right[g] - col[g - p] * row_r
        upper.append(jnp.where(lane >= sub + 8 * p, done_l, 0.0))
        inverse.append(done_r)
    return jnp.concatenate(upper, 0), jnp.concatenate(inverse, 0)


def dot_exact(a, b, contract):
    return lax.dot_general(
        a, b, (contract, ((), ())), precision=lax.Precision.HIGHEST, preferred_element_type=F32
    )


NT = ((1,), (1,))
NN = ((1,), (0,))


def factor_lead(work, pivots, inv):
    r = lax.broadcasted_iota(jnp.int32, (B, B), 0)
    c = lax.broadcasted_iota(jnp.int32, (B, B), 1)
    row_block = lax.broadcasted_iota(jnp.int32, (W, B), 0) // B
    col_block = lax.broadcasted_iota(jnp.int32, (B, W), 1) // B
    inv[...] = jnp.zeros_like(inv)

    def panel(k, _):
        at = pl.ds(pl.multiple_of(k * B, B), B)
        pivot = work[at, at]
        upper, inverse = factor_block(jnp.where(r >= c, pivot, pivot.T))
        pivots[k] = upper.T
        lower = jnp.where(row_block > k, dot_exact(work[:, at], inverse, NT), 0.0)
        before = jnp.where(col_block < k, work[at, :], 0.0)
        inv[at, :] = -dot_exact(inverse, dot_exact(before, inv[...], NN), NN)
        inv[at, at] = inverse
        work[...] = work[...] - dot_exact(lower, lower, NT)
        work[:, at] = lower
        return 0

    lax.fori_loop(0, PANELS, panel, 0)


def halves(a):
    high = a.astype(BF16)
    return high, (a - high.astype(F32)).astype(BF16)


def dot_split(a, b):
    (ah, al), (bh, bl) = a, b
    dot = functools.partial(
        lax.dot_general, dimension_numbers=(NT, ((), ())), preferred_element_type=F32
    )
    return dot(ah, bh) + (dot(al, bh) + dot(ah, bl))


STEP = 2


def finish_kernel(
    code, pattern, front, rows, match, pivots, arrived, out,
    inv_h, inv_l, across_h, across_l,
):
    n = pl.program_id(0)
    d = lax.axis_index("leaf")
    f = lax.axis_index("front")

    @pl.when(n == 0)
    def _():
        inv_h[...] = jnp.zeros_like(inv_h)
        inv_l[...] = jnp.zeros_like(inv_l)
        for i in range(PANELS):
            for j in range(i + 1):
                k = i * (i + 1) // 2 + j
                ks, ls = (CB + k // PANELS) * B, k % PANELS * B
                at, to = slice(i * B, i * B + B), slice(j * B, j * B + B)
                inv_h[at, to], inv_l[at, to] = halves(match[ks : ks + B, ls : ls + B])
        for i in range(0, CB, STEP):
            at = slice(i * B, (i + STEP) * B)
            lower = dot_split(halves(match[at, :]), (inv_h[...], inv_l[...]))
            across_h[at, :], across_l[at, :] = halves(lower)

    lower = dot_split(halves(rows[...]), (inv_h[...], inv_l[...]))
    product = dot_split(halves(lower), (across_h[...], across_l[...]))
    for rr in range(STEP):
        r = n * STEP + rr
        r_glob = d * RB + r
        rs = slice(rr * B, rr * B + B)
        for c in range(CB):
            c_glob = f * CB + c
            cs = slice(c * B, c * B + B)
            t = code[0, r * CB + c]
            keep = ((pattern[r, c] == 1) | (r_glob == c_glob)) & (r_glob >= c_glob)
            active = (r_glob >= c_glob) & (c_glob >= PANELS)
            block = arrived[jnp.maximum(t - 1, 0)]
            value = (front[rs, cs] + block * (t > 0).astype(F32)) * keep.astype(F32)
            out[rs, cs] = value - product[rs, cs] * active.astype(F32)

        @pl.when(f == 0)
        def _():
            for c in range(PANELS):
                cs = slice(c * B, c * B + B)
                out[rs, cs] = lower[rs, cs] * (r_glob > c).astype(F32)

                @pl.when(r_glob == c)
                def _():
                    out[rs, cs] = pivots[c]


def finish_call(code, pattern, front, rows, match, pivots, arrived):
    whole = lambda *shape: pl.BlockSpec(shape, lambda n, *_: (0,) * len(shape))
    return pl.pallas_call(
        finish_kernel,
        out_shape=jax.ShapeDtypeStruct(front.shape, F32),
        grid_spec=pltpu.PrefetchScalarGridSpec(
            num_scalar_prefetch=2,
            grid=(RB // STEP,),
            in_specs=[
                pl.BlockSpec((STEP * B, CB * B), lambda n, *_: (n, 0)),
                pl.BlockSpec((STEP * B, W), lambda n, *_: (n, 0)),
                whole(NR * B, W),
                whole(PANELS, B, B),
                whole(NL, B, B),
            ],
            out_specs=pl.BlockSpec((STEP * B, CB * B), lambda n, *_: (n, 0)),
            scratch_shapes=[
                pltpu.VMEM((W, W), BF16), pltpu.VMEM((W, W), BF16),
                pltpu.VMEM((CB * B, W), BF16), pltpu.VMEM((CB * B, W), BF16),
            ],
        ),
        compiler_params=pltpu.CompilerParams(vmem_limit_bytes=56 << 20),
    )(code, pattern, front, rows, match, pivots, arrived)


def body(front, child_blocks, child_map, pattern):
    child = child_blocks.reshape(NL, B, B)
    maptile = jnp.broadcast_to(child_map.reshape(NL, 1, 1), (NL, 8, B))
    arrived, code, rows, match, pivots = exchange_call(child, maptile, front, pattern)
    return finish_call(code, pattern, front, rows, match, pivots, arrived)


def solution(mesh):
    placed = (
        P("leaf", "front"),
        P("leaf", None, None, "front"),
        P("leaf", None, "front"),
        P("leaf", "front"),
    )
    return jax.shard_map(
        body, mesh=mesh, in_specs=placed, out_specs=P("leaf", "front"), check_vma=False
    )
```

```python
import functools

import jax
import jax.numpy as jnp
from jax import lax
from jax.experimental import pallas as pl
from jax.experimental.pallas import tpu as pltpu
from jax.sharding import PartitionSpec as P

B = 128
RB = 10
CB = 8
PANELS = 4
W = PANELS * B
NL = 32
NF = 8
NY = 4
NZ = 8
PIECE = B // NY
LR = PANELS
NR = CB + LR
NS = -(-NF * CB // RB)
LAG = 2
RELAY_LAG = 1
LEAD_TURN = CB
CHUNK = B // 2
NC = RB * B // CHUNK
F32 = jnp.float32
BF16 = jnp.bfloat16
MESH = pl.DeviceIdType.MESH
HBM = pl.BlockSpec(memory_space=pl.ANY)
SMEM = pl.BlockSpec(memory_space=pltpu.SMEM)
VMEM = pl.BlockSpec(memory_space=pltpu.VMEM)


def exchange(
    child, maptile, front, pattern,
    arrived_out, code, rows_out, match_out, pivots_out,
    child_v, arrived, front_v, rows, match, work, inv, pivots, map_v, code_v, code_s,
    a_send, a_recv, m_send, m_recv, x_send, x_recv, l_send, l_recv, t_send, t_recv,
    q_recv, qz_send, qy_send, qa_send, local,
):
    d = lax.axis_index("leaf")
    f = lax.axis_index("front")
    z, y = d // NY, d % NY
    x, core = f // 2, f % 2

    child_in = pltpu.make_async_copy(child, child_v, local.at[4])
    child_in.start()
    front_in = pltpu.make_async_copy(front.at[:, pl.ds(0, W)], front_v, local.at[3])

    @pl.when(f == 0)
    def _():
        front_in.start()

    barrier = pltpu.get_barrier_semaphore()

    def greet_leaf(k, _):
        pl.semaphore_signal(
            barrier, inc=1, device_id=(lax.rem(d + k, NL), f), device_id_type=MESH
        )
        return 0

    def greet_front(k, _):
        pl.semaphore_signal(
            barrier, inc=1, device_id=(d, lax.rem(f + k, NF)), device_id_type=MESH
        )
        return 0

    lax.fori_loop(1, NL, greet_leaf, 0)
    lax.fori_loop(1, NF, greet_front, 0)
    pl.semaphore_wait(barrier, NL - 1 + NF - 1)

    child_in.wait()

    def block_copy(to):
        return pltpu.make_async_remote_copy(
            src_ref=child_v.at[to], dst_ref=arrived.at[d], send_sem=a_send.at[to],
            recv_sem=a_recv.at[d], device_id=(to, f), device_id_type=MESH,
        )

    def map_copy(to):
        return pltpu.make_async_remote_copy(
            src_ref=maptile.at[to], dst_ref=map_v.at[d], send_sem=m_send.at[to],
            recv_sem=m_recv.at[d], device_id=(to, f), device_id_type=MESH,
        )

    def block_in(frm):
        return pltpu.make_async_remote_copy(
            src_ref=child_v.at[frm], dst_ref=arrived.at[frm], send_sem=a_send.at[frm],
            recv_sem=a_recv.at[frm], device_id=(frm, f), device_id_type=MESH,
        )

    def map_in(frm):
        return pltpu.make_async_remote_copy(
            src_ref=maptile.at[frm], dst_ref=map_v.at[frm], send_sem=m_send.at[frm],
            recv_sem=m_recv.at[frm], device_id=(frm, f), device_id_type=MESH,
        )

    own_block = pltpu.make_async_copy(child_v.at[d], arrived.at[d], local.at[0])
    own_map = pltpu.make_async_copy(maptile.at[d], map_v.at[d], local.at[1])

    def send_blocks():
        def step(k, _):
            early = jnp.where(k < NS, lax.rem(d + k, NS), NS + lax.rem(d + k, NL - NS))
            to = jnp.where(f == 0, early, lax.rem(d + k, NL))

            @pl.when(to != d)
            def _():
                map_copy(to).start()
                block_copy(to).start()

            return 0

        lax.fori_loop(0, NL, step, 0)

    def receive_blocks():
        def step(k, _):
            frm = lax.rem(d + k, NL)
            map_in(frm).wait_recv()
            block_in(frm).wait_recv()
            return 0

        lax.fori_loop(1, NL, step, 0)
        own_block.wait()
        own_map.wait()
        lane = lax.broadcasted_iota(jnp.int32, (8, B), 1)

        def latest(s, total):
            return jnp.maximum(total, jnp.where(map_v[s] == lane, s + 1, 0))

        code_v[...] = lax.fori_loop(0, NL, latest, jnp.zeros((8, B), jnp.int32))
        pltpu.make_async_copy(code_v, code, local.at[2]).start()
        pltpu.make_async_copy(arrived, arrived_out, local.at[0]).start()

    own_block.start()
    own_map.start()

    @pl.when(f != 1)
    def _():
        send_blocks()

    def chunk_of(j):
        return rows.at[pl.ds(pl.multiple_of(j * CHUNK, CHUNK), CHUNK)]

    def chunk_copy(j, to, way):
        return pltpu.make_async_remote_copy(
            src_ref=chunk_of(j), dst_ref=chunk_of(j), send_sem=x_send.at[j, way],
            recv_sem=x_recv.at[j], device_id=(d, to), device_id_type=MESH,
        )

    def root_next(j):
        return jnp.where(j % 2 == 0, 2, NF - 1)

    @pl.when(f == 0)
    def _():
        receive_blocks()
        to_smem = pltpu.make_async_copy(code_v, code_s, local.at[3])
        front_in.wait()
        to_smem.start()
        to_smem.wait()

        def form(r, _):
            r_glob = d * RB + r
            at = pl.ds(pl.multiple_of(r * B, B), B)
            for c in range(PANELS):
                t = code_s[0, r * CB + c]
                block = arrived[jnp.maximum(t - 1, 0)]
                has = (t > 0).astype(F32)
                keep = ((pattern[r, c] == 1) | (r_glob == c)) & (r_glob >= c)
                raw = front_v[at, c * B : (c + 1) * B]
                rows[at, c * B : (c + 1) * B] = (raw + block * has) * keep.astype(F32)
            for h in range(2):
                j = 2 * r + h
                chunk_copy(j, root_next(j), 0).start()
                chunk_copy(j, 1, 1).start()
            return 0

        lax.fori_loop(0, RB, form, 0)

    pair = f + 1 - 2 * core
    onward = f + 2 - 4 * core
    has_onward = ((core == 0) & (x < 3)) | ((core == 1) & (x > 1))

    def pass_on(n):
        j = 2 * n + core
        chunk_copy(j, 0, 0).wait_recv()

        @pl.when(f >= 2)
        def _():
            @pl.when(has_onward)
            def _():
                chunk_copy(j, onward, 0).start()

            chunk_copy(j, pair, 1).start()

        @pl.when((f == 1) & (n == 0))
        def _():
            send_blocks()

    def take_rest():
        def ending(n, _):
            chunk_copy(2 * n + 1 - core, 0, 0).wait_recv()
            return 0

        lax.fori_loop(0, NC // 2, ending, 0)

    def where_from(i, lead):
        r = 0 if lead else f * CB + i
        source = r // RB
        zs, ys = source // NY, source % NY
        return r % RB, ys, lax.rem(z - zs + NZ, NZ)

    def row_of(ref, i):
        return ref.at[pl.ds(pl.multiple_of(i * B, B), B)]

    def piece_of(ref, i, q):
        return ref.at[pl.ds(pl.multiple_of(i * B + q * PIECE, PIECE), PIECE)]

    def piece_copy(src, i, q, to_z, to_y, sem):
        return pltpu.make_async_remote_copy(
            src_ref=src, dst_ref=piece_of(match, i, q), send_sem=sem,
            recv_sem=q_recv.at[i, q], device_id=(to_z * NY + to_y, f), device_id_type=MESH,
        )

    def z_copy(src, i, up):
        to = lax.rem(z + (1 if up else NZ - 1), NZ)
        return piece_copy(src, i, y, to, y, qz_send.at[i, 0 if up else 1])

    def match_row(i, act, lead):
        r_loc, ys, zr = where_from(i, lead)
        held, r_at = (match, i) if lead else (rows, r_loc)
        at_source = (zr == 0) & (y == ys)

        @pl.when(at_source)
        def _():
            mine = piece_of(held, r_at, y)
            for k in range(1, NY):
                q = lax.rem(y + k, NY)
                act(piece_copy(piece_of(held, r_at, q), i, q, z, q, qa_send.at[i, k]))
            act(z_copy(mine, i, True))
            act(z_copy(mine, i, False))
            for k in (1, NY - 1):
                q = lax.rem(y + k, NY)
                act(piece_copy(mine, i, y, z, q, qy_send.at[i, k]))
            if not lead:
                act(
                    pltpu.make_async_copy(row_of(rows, r_loc), row_of(match, i), local.at[16 + i]),
                    here=True,
                )

        @pl.when(jnp.logical_not(at_source))
        def _():
            mine = piece_of(match, i, y)
            act(None, i, y)

            @pl.when(zr < NZ // 2)
            def _():
                act(z_copy(mine, i, True))

            @pl.when((zr == 0) | (zr > NZ // 2 + 1))
            def _():
                act(z_copy(mine, i, False))

            for k in (1, NY - 1):
                q = lax.rem(y + k, NY)

                @pl.when((zr != 0) | (q != ys))
                def _():
                    act(piece_copy(mine, i, y, z, q, qy_send.at[i, k]))

    def relay_row(i, act, lead):
        r_loc, ys, zr = where_from(i, lead)
        held, r_at = (match, i) if lead else (rows, r_loc)
        at_source = (zr == 0) & (y == ys)
        back = jnp.where(i % 2 == 0, NY - 1, 1)
        q, to = lax.rem(y + back, NY), lax.rem(y + NY - back, NY)

        @pl.when(at_source)
        def _():
            act(piece_copy(piece_of(held, r_at, q), i, q, z, to, qy_send.at[i, 0]))

        @pl.when(jnp.logical_not(at_source))
        def _():
            act(None, i, q)

            @pl.when((zr != 0) | (to != ys))
            def _():
                act(piece_copy(piece_of(match, i, q), i, q, z, to, qy_send.at[i, 0]))

            act(None, i, to, late=True)
            act(None, i, lax.rem(y + 2, NY), late=True)

    def piece_in(i, q):
        piece_copy(piece_of(match, i, q), i, q, z, lax.rem(y + 1, NY), qy_send.at[i, 1]).wait_recv()

    def begin(copy, i=None, q=None, late=False, here=False):
        if copy is not None:
            copy.start()
        elif not late:
            piece_in(i, q)

    def finish(copy, i=None, q=None, late=False, here=False):
        if copy is None:
            if late:
                piece_in(i, q)
        elif here:
            copy.wait()
        else:
            copy.wait_send()

    def run(turn, act, first, last, lead):
        def step(i, _):
            turn(i, act, lead)
            return 0

        lax.fori_loop(first, last, step, 0)

    def lead_copy(i, to, way):
        return pltpu.make_async_remote_copy(
            src_ref=row_of(match, i), dst_ref=row_of(match, i), send_sem=l_send.at[i - CB, way],
            recv_sem=l_recv.at[i - CB], device_id=(d, to), device_id_type=MESH,
        )

    def twin_copy(i, to):
        return pltpu.make_async_remote_copy(
            src_ref=row_of(match, i), dst_ref=row_of(match, i), send_sem=t_send.at[i - CB],
            recv_sem=t_recv.at[i - CB], device_id=(d, to), device_id_type=MESH,
        )

    is_root = (d == 0) & (f == 0)
    keep_pivots = pltpu.make_async_copy(pivots, pivots_out, local.at[6])

    def lead_done(k):
        match[pl.ds(pl.multiple_of((CB + k) * B, B), B), :] = inv[pl.ds(pl.multiple_of(k * B, B), B), :]
        lead_copy(CB + k, 2, 0).start()
        lead_copy(CB + k, NF - 2, 1).start()
        match_row(CB + k, begin, True)
        relay_row(CB + k, begin, True)

    def pass_lead(i):
        @pl.when((d == 0) & (f != 0))
        def _():
            lead_copy(i, 0, 0).wait_recv()

            @pl.when(f == 2)
            def _():
                lead_copy(i, 4, 0).start()

        match_row(i, begin, True)

    behind = jnp.where(f == 0, 0, jnp.where(d < NS, NC // 2, LAG))

    def turn(n, _):
        @pl.when((f != 0) & (n < NC // 2))
        def _():
            pass_on(n)

        @pl.when((f != 0) & (d < NS) & (n == NC // 2))
        def _():
            take_rest()

        m = n - behind

        @pl.when((m >= 0) & (m < CB))
        def _():
            match_row(m, begin, False)

        @pl.when((m >= RELAY_LAG) & (m < CB + RELAY_LAG))
        def _():
            relay_row(m - RELAY_LAG, begin, False)

        i = m - jnp.where(d == 0, jnp.where(f >= 5, -LR, 0), LEAD_TURN) + CB
        takes_lead = (core == 0) & jnp.logical_not(is_root)

        @pl.when(takes_lead & (i >= CB) & (i < NR))
        def _():
            pass_lead(i)

        @pl.when(takes_lead & (i >= CB + RELAY_LAG) & (i < NR + RELAY_LAG))
        def _():
            relay_row(i - RELAY_LAG, begin, True)

        return 0

    lax.fori_loop(0, NC // 2 + max(CB, LEAD_TURN + LR) + RELAY_LAG, turn, 0)

    @pl.when(is_root)
    def _():
        work[...] = rows[0:W, :]
        factor_lead(work, pivots, inv, lead_done)
        keep_pivots.start()

    @pl.when((f != 0) & (d >= NS))
    def _():
        take_rest()

    keep_rows = pltpu.make_async_copy(rows, rows_out, local.at[7])
    keep_rows.start()

    @pl.when(f != 0)
    def _():
        receive_blocks()

    run(match_row, finish, 0, CB, False)
    run(relay_row, finish, 0, CB, False)
    keep_match = pltpu.make_async_copy(
        match.at[pl.ds(0, CB * B)], match_out.at[pl.ds(0, CB * B)], local.at[5]
    )
    keep_match.start()

    @pl.when(core == 0)
    def _():
        run(match_row, finish, CB, NR, True)
        run(relay_row, finish, CB, NR, True)
        for i in range(CB, NR):
            twin_copy(i, f + 1).start()
        for i in range(CB, NR):
            twin_copy(i, f + 1).wait_send()

    @pl.when(core == 1)
    def _():
        for i in range(CB, NR):
            twin_copy(i, f - 1).wait_recv()

    keep_lead = pltpu.make_async_copy(
        match.at[pl.ds(CB * B, LR * B)], match_out.at[pl.ds(CB * B, LR * B)], local.at[8]
    )
    keep_lead.start()

    @pl.when(is_root)
    def _():
        for i in range(CB, NR):
            lead_copy(i, 2, 0).wait_send()
            lead_copy(i, NF - 2, 1).wait_send()
        keep_pivots.wait()

    @pl.when((d == 0) & (f == 2))
    def _():
        for i in range(CB, NR):
            lead_copy(i, 4, 0).wait_send()

    def sent(k, _):
        to = lax.rem(d + k, NL)
        map_copy(to).wait_send()
        block_copy(to).wait_send()
        return 0

    lax.fori_loop(1, NL, sent, 0)

    @pl.when(f == 0)
    def _():
        def chunk_sent(j, _):
            chunk_copy(j, root_next(j), 0).wait_send()
            chunk_copy(j, 1, 1).wait_send()
            return 0

        lax.fori_loop(0, NC, chunk_sent, 0)

    @pl.when(f >= 2)
    def _():
        def chunk_sent(n, _):
            j = 2 * n + core

            @pl.when(has_onward)
            def _():
                chunk_copy(j, onward, 0).wait_send()

            chunk_copy(j, pair, 1).wait_send()
            return 0

        lax.fori_loop(0, NC // 2, chunk_sent, 0)

    keep_rows.wait()
    keep_match.wait()
    keep_lead.wait()
    pltpu.make_async_copy(code_v, code, local.at[2]).wait()
    pltpu.make_async_copy(arrived, arrived_out, local.at[0]).wait()


def exchange_call(child, maptile, front, pattern):
    dma = pltpu.SemaphoreType.DMA
    shape = jax.ShapeDtypeStruct
    return pl.pallas_call(
        exchange,
        out_shape=(
            shape((NL, B, B), F32), shape((8, B), jnp.int32),
            shape((RB * B, W), F32), shape((NR * B, W), F32), shape((PANELS, B, B), F32),
        ),
        in_specs=[HBM, HBM, HBM, SMEM],
        out_specs=(HBM,) * 5,
        scratch_shapes=[
            pltpu.VMEM((NL, B, B), F32), pltpu.VMEM((NL, B, B), F32),
            pltpu.VMEM((RB * B, W), F32), pltpu.VMEM((RB * B, W), F32),
            pltpu.VMEM((NR * B, W), F32), pltpu.VMEM((W, W), F32), pltpu.VMEM((W, W), F32),
            pltpu.VMEM((PANELS, B, B), F32), pltpu.VMEM((NL, 8, B), jnp.int32),
            pltpu.VMEM((8, B), jnp.int32), pltpu.SMEM((8, B), jnp.int32),
            dma((NL,)), dma((NL,)), dma((NL,)), dma((NL,)), dma((NC, 2)), dma((NC,)),
            dma((LR, 2)), dma((LR,)), dma((LR,)), dma((LR,)),
            dma((NR, NY)), dma((NR, 2)), dma((NR, NY)), dma((NR, NY)), dma((16 + NR,)),
        ],
        compiler_params=pltpu.CompilerParams(
            collective_id=0, has_side_effects=True, vmem_limit_bytes=56 << 20
        ),
    )(child, maptile, front, pattern)


def factor_block(s):
    sub = lax.broadcasted_iota(jnp.int32, (8, B), 0)
    lane = lax.broadcasted_iota(jnp.int32, (8, B), 1)
    groups = B // 8

    def down(value, i):
        return jnp.broadcast_to(value[i : i + 1, :], (8, B))

    left = [s[8 * g : 8 * g + 8, :] for g in range(groups)]
    right = [(lane == sub + 8 * g).astype(F32) for g in range(groups)]
    upper, inverse = [], []
    for p in range(groups):
        cols = [
            [jnp.broadcast_to(left[g][:, 8 * p + i : 8 * p + i + 1], (8, B)) for g in range(p, groups)]
            for i in range(8)
        ]
        done_l = jnp.zeros((8, B), F32)
        done_r = jnp.zeros((8, B), F32)
        for i in range(8):
            scale = lax.rsqrt(down(cols[i][0], i))
            col = [value * scale for value in cols[i]]
            row_l = down(left[p], i) * scale
            row_r = down(right[p], i) * scale
            done_l = jnp.where(sub == i, row_l, done_l)
            done_r = jnp.where(sub == i, row_r, done_r)
            for k in range(i + 1, 8):
                at = down(col[0], k)
                cols[k] = [v - w * at for v, w in zip(cols[k], col)]
            for g in range(p, groups):
                left[g] = left[g] - col[g - p] * row_l
                right[g] = right[g] - col[g - p] * row_r
        upper.append(jnp.where(lane >= sub + 8 * p, done_l, 0.0))
        inverse.append(done_r)
    return jnp.concatenate(upper, 0), jnp.concatenate(inverse, 0)


def dot_exact(a, b, contract):
    return lax.dot_general(
        a, b, (contract, ((), ())), precision=lax.Precision.HIGHEST, preferred_element_type=F32
    )


NT = ((1,), (1,))
NN = ((1,), (0,))


def factor_lead(work, pivots, inv, done):
    r = lax.broadcasted_iota(jnp.int32, (B, B), 0)
    c = lax.broadcasted_iota(jnp.int32, (B, B), 1)
    row_block = lax.broadcasted_iota(jnp.int32, (W, B), 0) // B
    col_block = lax.broadcasted_iota(jnp.int32, (B, W), 1) // B
    inv[...] = jnp.zeros_like(inv)

    def panel(k, _):
        at = pl.ds(pl.multiple_of(k * B, B), B)
        pivot = work[at, at]
        upper, inverse = factor_block(jnp.where(r >= c, pivot, pivot.T))
        pivots[k] = upper.T
        lower = jnp.where(row_block > k, dot_exact(work[:, at], inverse, NT), 0.0)
        before = jnp.where(col_block < k, work[at, :], 0.0)
        inv[at, :] = -dot_exact(inverse, dot_exact(before, inv[...], NN), NN)
        inv[at, at] = inverse
        done(k)
        work[...] = work[...] - dot_exact(lower, lower, NT)
        work[:, at] = lower
        return 0

    lax.fori_loop(0, PANELS, panel, 0)


def halves(a):
    high = a.astype(BF16)
    return high, (a - high.astype(F32)).astype(BF16)


def dot_split(a, b):
    (ah, al), (bh, bl) = a, b
    dot = functools.partial(
        lax.dot_general, dimension_numbers=(NT, ((), ())), preferred_element_type=F32
    )
    return dot(ah, bh) + (dot(al, bh) + dot(ah, bl))


STEP = 2


def finish_kernel(
    code, pattern, front, rows, match, pivots, arrived, out,
    inv_h, inv_l, across_h, across_l,
):
    n = pl.program_id(0)
    d = lax.axis_index("leaf")
    f = lax.axis_index("front")

    @pl.when(n == 0)
    def _():
        inv_h[...], inv_l[...] = halves(match[CB * B :, :])
        for i in range(0, CB, STEP):
            at = slice(i * B, (i + STEP) * B)
            lower = dot_split(halves(match[at, :]), (inv_h[...], inv_l[...]))
            across_h[at, :], across_l[at, :] = halves(lower)

    lower = dot_split(halves(rows[...]), (inv_h[...], inv_l[...]))
    product = dot_split(halves(lower), (across_h[...], across_l[...]))
    for rr in range(STEP):
        r = n * STEP + rr
        r_glob = d * RB + r
        rs = slice(rr * B, rr * B + B)
        for c in range(CB):
            c_glob = f * CB + c
            cs = slice(c * B, c * B + B)
            t = code[0, r * CB + c]
            keep = ((pattern[r, c] == 1) | (r_glob == c_glob)) & (r_glob >= c_glob)
            active = (r_glob >= c_glob) & (c_glob >= PANELS)
            block = arrived[jnp.maximum(t - 1, 0)]
            value = (front[rs, cs] + block * (t > 0).astype(F32)) * keep.astype(F32)
            out[rs, cs] = value - product[rs, cs] * active.astype(F32)

        @pl.when(f == 0)
        def _():
            for c in range(PANELS):
                cs = slice(c * B, c * B + B)
                out[rs, cs] = lower[rs, cs] * (r_glob > c).astype(F32)

                @pl.when(r_glob == c)
                def _():
                    out[rs, cs] = pivots[c]


def finish_call(code, pattern, front, rows, match, pivots, arrived):
    whole = lambda *shape: pl.BlockSpec(shape, lambda n, *_: (0,) * len(shape))
    return pl.pallas_call(
        finish_kernel,
        out_shape=jax.ShapeDtypeStruct(front.shape, F32),
        grid_spec=pltpu.PrefetchScalarGridSpec(
            num_scalar_prefetch=2,
            grid=(RB // STEP,),
            in_specs=[
                pl.BlockSpec((STEP * B, CB * B), lambda n, *_: (n, 0)),
                pl.BlockSpec((STEP * B, W), lambda n, *_: (n, 0)),
                whole(NR * B, W),
                whole(PANELS, B, B),
                whole(NL, B, B),
            ],
            out_specs=pl.BlockSpec((STEP * B, CB * B), lambda n, *_: (n, 0)),
            scratch_shapes=[
                pltpu.VMEM((W, W), BF16), pltpu.VMEM((W, W), BF16),
                pltpu.VMEM((CB * B, W), BF16), pltpu.VMEM((CB * B, W), BF16),
            ],
        ),
        compiler_params=pltpu.CompilerParams(vmem_limit_bytes=56 << 20),
    )(code, pattern, front, rows, match, pivots, arrived)


def body(front, child_blocks, child_map, pattern):
    child = child_blocks.reshape(NL, B, B)
    maptile = jnp.broadcast_to(child_map.reshape(NL, 1, 1), (NL, 8, B))
    arrived, code, rows, match, pivots = exchange_call(child, maptile, front, pattern)
    return finish_call(code, pattern, front, rows, match, pivots, arrived)


def solution(mesh):
    placed = (
        P("leaf", "front"),
        P("leaf", None, None, "front"),
        P("leaf", None, "front"),
        P("leaf", "front"),
    )
    return jax.shard_map(
        body, mesh=mesh, in_specs=placed, out_specs=P("leaf", "front"), check_vma=False
    )
```

```python
import functools

import jax
import jax.numpy as jnp
from jax import lax
from jax.experimental import pallas as pl
from jax.experimental.pallas import tpu as pltpu
from jax.sharding import PartitionSpec as P

B = 128
RB = 10
CB = 8
PANELS = 4
W = PANELS * B
NL = 32
NF = 8
NY = 4
NZ = 8
PIECE = B // NY
LR = PANELS
NR = CB + LR
NS = -(-NF * CB // RB)
LAG = 2
RELAY_LAG = 1
LEAD_TURN = CB
CHUNK = B // 2
NC = RB * B // CHUNK
F32 = jnp.float32
BF16 = jnp.bfloat16
MESH = pl.DeviceIdType.MESH
HBM = pl.BlockSpec(memory_space=pl.ANY)
SMEM = pl.BlockSpec(memory_space=pltpu.SMEM)
VMEM = pl.BlockSpec(memory_space=pltpu.VMEM)


def exchange(
    child, maptile, front, pattern,
    arrived_out, code, rows_out, match_out, pivots_out,
    child_v, arrived, front_v, rows, match, work, inv, pivots, map_v, code_v, code_s,
    a_send, a_recv, m_send, m_recv, x_send, x_recv, l_send, l_recv, t_send, t_recv,
    q_recv, qz_send, qy_send, qa_send, local,
):
    d = lax.axis_index("leaf")
    f = lax.axis_index("front")
    z, y = d // NY, d % NY
    x, core = f // 2, f % 2

    child_in = pltpu.make_async_copy(child, child_v, local.at[4])
    child_in.start()
    front_in = pltpu.make_async_copy(front.at[:, pl.ds(0, W)], front_v, local.at[3])

    @pl.when(f == 0)
    def _():
        front_in.start()

    barrier = pltpu.get_barrier_semaphore()

    def greet_leaf(k, _):
        pl.semaphore_signal(
            barrier, inc=1, device_id=(lax.rem(d + k, NL), f), device_id_type=MESH
        )
        return 0

    def greet_front(k, _):
        pl.semaphore_signal(
            barrier, inc=1, device_id=(d, lax.rem(f + k, NF)), device_id_type=MESH
        )
        return 0

    lax.fori_loop(1, NL, greet_leaf, 0)
    lax.fori_loop(1, NF, greet_front, 0)
    pl.semaphore_wait(barrier, NL - 1 + NF - 1)

    child_in.wait()

    def block_copy(to):
        return pltpu.make_async_remote_copy(
            src_ref=child_v.at[to], dst_ref=arrived.at[d], send_sem=a_send.at[to],
            recv_sem=a_recv.at[d], device_id=(to, f), device_id_type=MESH,
        )

    def map_copy(to):
        return pltpu.make_async_remote_copy(
            src_ref=maptile.at[to], dst_ref=map_v.at[d], send_sem=m_send.at[to],
            recv_sem=m_recv.at[d], device_id=(to, f), device_id_type=MESH,
        )

    def block_in(frm):
        return pltpu.make_async_remote_copy(
            src_ref=child_v.at[frm], dst_ref=arrived.at[frm], send_sem=a_send.at[frm],
            recv_sem=a_recv.at[frm], device_id=(frm, f), device_id_type=MESH,
        )

    def map_in(frm):
        return pltpu.make_async_remote_copy(
            src_ref=maptile.at[frm], dst_ref=map_v.at[frm], send_sem=m_send.at[frm],
            recv_sem=m_recv.at[frm], device_id=(frm, f), device_id_type=MESH,
        )

    own_block = pltpu.make_async_copy(child_v.at[d], arrived.at[d], local.at[0])
    own_map = pltpu.make_async_copy(maptile.at[d], map_v.at[d], local.at[1])

    def send_blocks():
        def step(k, _):
            early = jnp.where(k < NS, lax.rem(d + k, NS), NS + lax.rem(d + k, NL - NS))
            to = jnp.where(f == 0, early, lax.rem(d + k, NL))

            @pl.when(to != d)
            def _():
                map_copy(to).start()
                block_copy(to).start()

            return 0

        lax.fori_loop(0, NL, step, 0)

    def receive_blocks():
        def step(k, _):
            frm = lax.rem(d + k, NL)
            map_in(frm).wait_recv()
            block_in(frm).wait_recv()
            return 0

        lax.fori_loop(1, NL, step, 0)
        own_block.wait()
        own_map.wait()
        lane = lax.broadcasted_iota(jnp.int32, (8, B), 1)

        def latest(s, total):
            return jnp.maximum(total, jnp.where(map_v[s] == lane, s + 1, 0))

        code_v[...] = lax.fori_loop(0, NL, latest, jnp.zeros((8, B), jnp.int32))
        pltpu.make_async_copy(code_v, code, local.at[2]).start()
        pltpu.make_async_copy(arrived, arrived_out, local.at[0]).start()

    own_block.start()
    own_map.start()

    @pl.when(f != 1)
    def _():
        send_blocks()

    def chunk_of(j):
        return rows.at[pl.ds(pl.multiple_of(j * CHUNK, CHUNK), CHUNK)]

    def chunk_copy(j, to, way):
        return pltpu.make_async_remote_copy(
            src_ref=chunk_of(j), dst_ref=chunk_of(j), send_sem=x_send.at[j, way],
            recv_sem=x_recv.at[j], device_id=(d, to), device_id_type=MESH,
        )

    def root_next(j):
        return jnp.where(j % 2 == 0, 2, NF - 1)

    @pl.when(f == 0)
    def _():
        receive_blocks()
        to_smem = pltpu.make_async_copy(code_v, code_s, local.at[3])
        front_in.wait()
        to_smem.start()
        to_smem.wait()

        def form(r, _):
            r_glob = d * RB + r
            at = pl.ds(pl.multiple_of(r * B, B), B)
            for c in range(PANELS):
                t = code_s[0, r * CB + c]
                block = arrived[jnp.maximum(t - 1, 0)]
                has = (t > 0).astype(F32)
                keep = ((pattern[r, c] == 1) | (r_glob == c)) & (r_glob >= c)
                raw = front_v[at, c * B : (c + 1) * B]
                rows[at, c * B : (c + 1) * B] = (raw + block * has) * keep.astype(F32)
            for h in range(2):
                j = 2 * r + h
                chunk_copy(j, root_next(j), 0).start()
                chunk_copy(j, 1, 1).start()
            return 0

        lax.fori_loop(0, RB, form, 0)

    pair = f + 1 - 2 * core
    onward = f + 2 - 4 * core
    has_onward = ((core == 0) & (x < 3)) | ((core == 1) & (x > 1))

    def pass_on(n):
        j = 2 * n + core
        chunk_copy(j, 0, 0).wait_recv()

        @pl.when(f >= 2)
        def _():
            @pl.when(has_onward)
            def _():
                chunk_copy(j, onward, 0).start()

            chunk_copy(j, pair, 1).start()

        @pl.when((f == 1) & (n == 0))
        def _():
            send_blocks()

    def take_rest():
        def ending(n, _):
            chunk_copy(2 * n + 1 - core, 0, 0).wait_recv()
            return 0

        lax.fori_loop(0, NC // 2, ending, 0)

    def where_from(i, lead):
        r = 0 if lead else f * CB + i
        source = r // RB
        zs, ys = source // NY, source % NY
        return r % RB, ys, lax.rem(z - zs + NZ, NZ)

    def row_of(ref, i):
        return ref.at[pl.ds(pl.multiple_of(i * B, B), B)]

    def piece_of(ref, i, q):
        return ref.at[pl.ds(pl.multiple_of(i * B + q * PIECE, PIECE), PIECE)]

    def piece_copy(src, i, q, to_z, to_y, sem):
        return pltpu.make_async_remote_copy(
            src_ref=src, dst_ref=piece_of(match, i, q), send_sem=sem,
            recv_sem=q_recv.at[i, q], device_id=(to_z * NY + to_y, f), device_id_type=MESH,
        )

    def z_copy(src, i, up):
        to = lax.rem(z + (1 if up else NZ - 1), NZ)
        return piece_copy(src, i, y, to, y, qz_send.at[i, 0 if up else 1])

    def match_row(i, act, lead):
        r_loc, ys, zr = where_from(i, lead)
        held, r_at = (match, i) if lead else (rows, r_loc)
        at_source = (zr == 0) & (y == ys)

        @pl.when(at_source)
        def _():
            mine = piece_of(held, r_at, y)
            for k in range(1, NY):
                q = lax.rem(y + k, NY)
                act(piece_copy(piece_of(held, r_at, q), i, q, z, q, qa_send.at[i, k]))
            act(z_copy(mine, i, True))
            act(z_copy(mine, i, False))
            for k in (1, NY - 1):
                q = lax.rem(y + k, NY)
                act(piece_copy(mine, i, y, z, q, qy_send.at[i, k]))
            if not lead:
                act(
                    pltpu.make_async_copy(row_of(rows, r_loc), row_of(match, i), local.at[16 + i]),
                    here=True,
                )

        @pl.when(jnp.logical_not(at_source))
        def _():
            mine = piece_of(match, i, y)
            act(None, i, y)

            @pl.when(zr < NZ // 2)
            def _():
                act(z_copy(mine, i, True))

            @pl.when((zr == 0) | (zr > NZ // 2 + 1))
            def _():
                act(z_copy(mine, i, False))

            for k in (1, NY - 1):
                q = lax.rem(y + k, NY)

                @pl.when((zr != 0) | (q != ys))
                def _():
                    act(piece_copy(mine, i, y, z, q, qy_send.at[i, k]))

    def relay_row(i, act, lead):
        r_loc, ys, zr = where_from(i, lead)
        held, r_at = (match, i) if lead else (rows, r_loc)
        at_source = (zr == 0) & (y == ys)
        back = jnp.where(i % 2 == 0, NY - 1, 1)
        q, to = lax.rem(y + back, NY), lax.rem(y + NY - back, NY)

        @pl.when(at_source)
        def _():
            act(piece_copy(piece_of(held, r_at, q), i, q, z, to, qy_send.at[i, 0]))

        @pl.when(jnp.logical_not(at_source))
        def _():
            act(None, i, q)

            @pl.when((zr != 0) | (to != ys))
            def _():
                act(piece_copy(piece_of(match, i, q), i, q, z, to, qy_send.at[i, 0]))

            act(None, i, to, late=True)
            act(None, i, lax.rem(y + 2, NY), late=True)

    def piece_in(i, q):
        piece_copy(piece_of(match, i, q), i, q, z, lax.rem(y + 1, NY), qy_send.at[i, 1]).wait_recv()

    def begin(copy, i=None, q=None, late=False, here=False):
        if copy is not None:
            copy.start()
        elif not late:
            piece_in(i, q)

    def finish(copy, i=None, q=None, late=False, here=False):
        if copy is None:
            if late:
                piece_in(i, q)
        elif here:
            copy.wait()
        else:
            copy.wait_send()

    def run(turn, act, first, last, lead):
        def step(i, _):
            turn(i, act, lead)
            return 0

        lax.fori_loop(first, last, step, 0)

    def lead_copy(i, to, way):
        return pltpu.make_async_remote_copy(
            src_ref=row_of(match, i), dst_ref=row_of(match, i), send_sem=l_send.at[i - CB, way],
            recv_sem=l_recv.at[i - CB], device_id=(d, to), device_id_type=MESH,
        )

    def twin_copy(i, to):
        return pltpu.make_async_remote_copy(
            src_ref=row_of(match, i), dst_ref=row_of(match, i), send_sem=t_send.at[i - CB],
            recv_sem=t_recv.at[i - CB], device_id=(d, to), device_id_type=MESH,
        )

    is_root = (d == 0) & (f == 0)
    keep_pivots = pltpu.make_async_copy(pivots, pivots_out, local.at[6])

    def lead_done(k):
        match[pl.ds(pl.multiple_of((CB + k) * B, B), B), :] = inv[pl.ds(pl.multiple_of(k * B, B), B), :]
        lead_copy(CB + k, 2, 0).start()
        lead_copy(CB + k, NF - 2, 1).start()
        match_row(CB + k, begin, True)
        relay_row(CB + k, begin, True)

    def pass_lead(i):
        @pl.when((d == 0) & (f != 0))
        def _():
            lead_copy(i, 0, 0).wait_recv()

            @pl.when(f == 2)
            def _():
                lead_copy(i, 4, 0).start()

        match_row(i, begin, True)

    behind = jnp.where(f == 0, 0, jnp.where(d < NS, NC // 2, LAG))

    def turn(n, _):
        @pl.when((f != 0) & (n < NC // 2))
        def _():
            pass_on(n)

        @pl.when((f != 0) & (d < NS) & (n == NC // 2))
        def _():
            take_rest()

        m = n - behind

        @pl.when((m >= 0) & (m < CB))
        def _():
            match_row(m, begin, False)

        @pl.when((m >= RELAY_LAG) & (m < CB + RELAY_LAG))
        def _():
            relay_row(m - RELAY_LAG, begin, False)

        late = jnp.where(d == 0, 0, LEAD_TURN)
        i = m - jnp.where((f >= 5) & (d < NY), -LR, late) + CB
        takes_lead = (core == 0) & jnp.logical_not(is_root)

        @pl.when(takes_lead & (i >= CB) & (i < NR))
        def _():
            pass_lead(i)

        @pl.when(takes_lead & (i >= CB + RELAY_LAG) & (i < NR + RELAY_LAG))
        def _():
            relay_row(i - RELAY_LAG, begin, True)

        return 0

    lax.fori_loop(0, NC // 2 + max(CB, LEAD_TURN + LR) + RELAY_LAG, turn, 0)

    @pl.when(is_root)
    def _():
        work[...] = rows[0:W, :]
        factor_lead(work, pivots, inv, lead_done)
        keep_pivots.start()

    @pl.when((f != 0) & (d >= NS))
    def _():
        take_rest()

    keep_rows = pltpu.make_async_copy(rows, rows_out, local.at[7])
    keep_rows.start()

    @pl.when(f != 0)
    def _():
        receive_blocks()

    run(match_row, finish, 0, CB, False)
    run(relay_row, finish, 0, CB, False)
    keep_match = pltpu.make_async_copy(
        match.at[pl.ds(0, CB * B)], match_out.at[pl.ds(0, CB * B)], local.at[5]
    )
    keep_match.start()

    @pl.when(core == 0)
    def _():
        def hand_over(i, _):
            match_row(i, finish, True)
            relay_row(i, finish, True)
            twin_copy(i, f + 1).start()
            return 0

        lax.fori_loop(CB, NR, hand_over, 0)
        for i in range(CB, NR):
            twin_copy(i, f + 1).wait_send()

    @pl.when(core == 1)
    def _():
        for i in range(CB, NR):
            twin_copy(i, f - 1).wait_recv()

    keep_lead = pltpu.make_async_copy(
        match.at[pl.ds(CB * B, LR * B)], match_out.at[pl.ds(CB * B, LR * B)], local.at[8]
    )
    keep_lead.start()

    @pl.when(is_root)
    def _():
        for i in range(CB, NR):
            lead_copy(i, 2, 0).wait_send()
            lead_copy(i, NF - 2, 1).wait_send()
        keep_pivots.wait()

    @pl.when((d == 0) & (f == 2))
    def _():
        for i in range(CB, NR):
            lead_copy(i, 4, 0).wait_send()

    def sent(k, _):
        to = lax.rem(d + k, NL)
        map_copy(to).wait_send()
        block_copy(to).wait_send()
        return 0

    lax.fori_loop(1, NL, sent, 0)

    @pl.when(f == 0)
    def _():
        def chunk_sent(j, _):
            chunk_copy(j, root_next(j), 0).wait_send()
            chunk_copy(j, 1, 1).wait_send()
            return 0

        lax.fori_loop(0, NC, chunk_sent, 0)

    @pl.when(f >= 2)
    def _():
        def chunk_sent(n, _):
            j = 2 * n + core

            @pl.when(has_onward)
            def _():
                chunk_copy(j, onward, 0).wait_send()

            chunk_copy(j, pair, 1).wait_send()
            return 0

        lax.fori_loop(0, NC // 2, chunk_sent, 0)

    keep_rows.wait()
    keep_match.wait()
    keep_lead.wait()
    pltpu.make_async_copy(code_v, code, local.at[2]).wait()
    pltpu.make_async_copy(arrived, arrived_out, local.at[0]).wait()


def exchange_call(child, maptile, front, pattern):
    dma = pltpu.SemaphoreType.DMA
    shape = jax.ShapeDtypeStruct
    return pl.pallas_call(
        exchange,
        out_shape=(
            shape((NL, B, B), F32), shape((8, B), jnp.int32),
            shape((RB * B, W), F32), shape((NR * B, W), F32), shape((PANELS, B, B), F32),
        ),
        in_specs=[HBM, HBM, HBM, SMEM],
        out_specs=(HBM,) * 5,
        scratch_shapes=[
            pltpu.VMEM((NL, B, B), F32), pltpu.VMEM((NL, B, B), F32),
            pltpu.VMEM((RB * B, W), F32), pltpu.VMEM((RB * B, W), F32),
            pltpu.VMEM((NR * B, W), F32), pltpu.VMEM((W, W), F32), pltpu.VMEM((W, W), F32),
            pltpu.VMEM((PANELS, B, B), F32), pltpu.VMEM((NL, 8, B), jnp.int32),
            pltpu.VMEM((8, B), jnp.int32), pltpu.SMEM((8, B), jnp.int32),
            dma((NL,)), dma((NL,)), dma((NL,)), dma((NL,)), dma((NC, 2)), dma((NC,)),
            dma((LR, 2)), dma((LR,)), dma((LR,)), dma((LR,)),
            dma((NR, NY)), dma((NR, 2)), dma((NR, NY)), dma((NR, NY)), dma((16 + NR,)),
        ],
        compiler_params=pltpu.CompilerParams(
            collective_id=0, has_side_effects=True, vmem_limit_bytes=56 << 20
        ),
    )(child, maptile, front, pattern)


def factor_block(s):
    sub = lax.broadcasted_iota(jnp.int32, (8, B), 0)
    lane = lax.broadcasted_iota(jnp.int32, (8, B), 1)
    groups = B // 8

    def down(value, i):
        return jnp.broadcast_to(value[i : i + 1, :], (8, B))

    left = [s[8 * g : 8 * g + 8, :] for g in range(groups)]
    right = [(lane == sub + 8 * g).astype(F32) for g in range(groups)]
    upper, inverse = [], []
    for p in range(groups):
        cols = [
            [jnp.broadcast_to(left[g][:, 8 * p + i : 8 * p + i + 1], (8, B)) for g in range(p, groups)]
            for i in range(8)
        ]
        done_l = jnp.zeros((8, B), F32)
        done_r = jnp.zeros((8, B), F32)
        for i in range(8):
            scale = lax.rsqrt(down(cols[i][0], i))
            col = [value * scale for value in cols[i]]
            row_l = down(left[p], i) * scale
            row_r = down(right[p], i) * scale
            done_l = jnp.where(sub == i, row_l, done_l)
            done_r = jnp.where(sub == i, row_r, done_r)
            for k in range(i + 1, 8):
                at = down(col[0], k)
                cols[k] = [v - w * at for v, w in zip(cols[k], col)]
            for g in range(p, groups):
                left[g] = left[g] - col[g - p] * row_l
                right[g] = right[g] - col[g - p] * row_r
        upper.append(jnp.where(lane >= sub + 8 * p, done_l, 0.0))
        inverse.append(done_r)
    return jnp.concatenate(upper, 0), jnp.concatenate(inverse, 0)


def dot_exact(a, b, contract):
    return lax.dot_general(
        a, b, (contract, ((), ())), precision=lax.Precision.HIGHEST, preferred_element_type=F32
    )


NT = ((1,), (1,))
NN = ((1,), (0,))


def factor_lead(work, pivots, inv, done):
    r = lax.broadcasted_iota(jnp.int32, (B, B), 0)
    c = lax.broadcasted_iota(jnp.int32, (B, B), 1)
    row_block = lax.broadcasted_iota(jnp.int32, (W, B), 0) // B
    col_block = lax.broadcasted_iota(jnp.int32, (B, W), 1) // B
    inv[...] = jnp.zeros_like(inv)

    def panel(k, _):
        at = pl.ds(pl.multiple_of(k * B, B), B)
        pivot = work[at, at]
        upper, inverse = factor_block(jnp.where(r >= c, pivot, pivot.T))
        pivots[k] = upper.T
        lower = jnp.where(row_block > k, dot_exact(work[:, at], inverse, NT), 0.0)
        before = jnp.where(col_block < k, work[at, :], 0.0)
        inv[at, :] = -dot_exact(inverse, dot_exact(before, inv[...], NN), NN)
        inv[at, at] = inverse
        done(k)
        work[...] = work[...] - dot_exact(lower, lower, NT)
        work[:, at] = lower
        return 0

    lax.fori_loop(0, PANELS, panel, 0)


def halves(a):
    high = a.astype(BF16)
    return high, (a - high.astype(F32)).astype(BF16)


def dot_split(a, b):
    (ah, al), (bh, bl) = a, b
    dot = functools.partial(
        lax.dot_general, dimension_numbers=(NT, ((), ())), preferred_element_type=F32
    )
    return dot(ah, bh) + (dot(al, bh) + dot(ah, bl))


STEP = 2


def finish_kernel(
    code, pattern, front, rows, match, pivots, arrived, out,
    inv_h, inv_l, across_h, across_l,
):
    n = pl.program_id(0)
    d = lax.axis_index("leaf")
    f = lax.axis_index("front")

    @pl.when(n == 0)
    def _():
        inv_h[...], inv_l[...] = halves(match[CB * B :, :])
        for i in range(0, CB, STEP):
            at = slice(i * B, (i + STEP) * B)
            lower = dot_split(halves(match[at, :]), (inv_h[...], inv_l[...]))
            across_h[at, :], across_l[at, :] = halves(lower)

    lower = dot_split(halves(rows[...]), (inv_h[...], inv_l[...]))
    product = dot_split(halves(lower), (across_h[...], across_l[...]))
    for rr in range(STEP):
        r = n * STEP + rr
        r_glob = d * RB + r
        rs = slice(rr * B, rr * B + B)
        for c in range(CB):
            c_glob = f * CB + c
            cs = slice(c * B, c * B + B)
            t = code[0, r * CB + c]
            keep = ((pattern[r, c] == 1) | (r_glob == c_glob)) & (r_glob >= c_glob)
            active = (r_glob >= c_glob) & (c_glob >= PANELS)
            block = arrived[jnp.maximum(t - 1, 0)]
            value = (front[rs, cs] + block * (t > 0).astype(F32)) * keep.astype(F32)
            out[rs, cs] = value - product[rs, cs] * active.astype(F32)

        @pl.when(f == 0)
        def _():
            for c in range(PANELS):
                cs = slice(c * B, c * B + B)
                out[rs, cs] = lower[rs, cs] * (r_glob > c).astype(F32)

                @pl.when(r_glob == c)
                def _():
                    out[rs, cs] = pivots[c]


def finish_call(code, pattern, front, rows, match, pivots, arrived):
    whole = lambda *shape: pl.BlockSpec(shape, lambda n, *_: (0,) * len(shape))
    return pl.pallas_call(
        finish_kernel,
        out_shape=jax.ShapeDtypeStruct(front.shape, F32),
        grid_spec=pltpu.PrefetchScalarGridSpec(
            num_scalar_prefetch=2,
            grid=(RB // STEP,),
            in_specs=[
                pl.BlockSpec((STEP * B, CB * B), lambda n, *_: (n, 0)),
                pl.BlockSpec((STEP * B, W), lambda n, *_: (n, 0)),
                whole(NR * B, W),
                whole(PANELS, B, B),
                whole(NL, B, B),
            ],
            out_specs=pl.BlockSpec((STEP * B, CB * B), lambda n, *_: (n, 0)),
            scratch_shapes=[
                pltpu.VMEM((W, W), BF16), pltpu.VMEM((W, W), BF16),
                pltpu.VMEM((CB * B, W), BF16), pltpu.VMEM((CB * B, W), BF16),
            ],
        ),
        compiler_params=pltpu.CompilerParams(vmem_limit_bytes=56 << 20),
    )(code, pattern, front, rows, match, pivots, arrived)


def body(front, child_blocks, child_map, pattern):
    child = child_blocks.reshape(NL, B, B)
    maptile = jnp.broadcast_to(child_map.reshape(NL, 1, 1), (NL, 8, B))
    arrived, code, rows, match, pivots = exchange_call(child, maptile, front, pattern)
    return finish_call(code, pattern, front, rows, match, pivots, arrived)


def solution(mesh):
    placed = (
        P("leaf", "front"),
        P("leaf", None, None, "front"),
        P("leaf", None, "front"),
        P("leaf", "front"),
    )
    return jax.shard_map(
        body, mesh=mesh, in_specs=placed, out_specs=P("leaf", "front"), check_vma=False
    )
```

```python
import functools

import jax
import jax.numpy as jnp
from jax import lax
from jax.experimental import pallas as pl
from jax.experimental.pallas import tpu as pltpu
from jax.sharding import PartitionSpec as P

B = 128
RB = 10
CB = 8
PANELS = 4
W = PANELS * B
NL = 32
NF = 8
NY = 4
NZ = 8
PIECE = B // NY
LR = PANELS
NR = CB + LR
NS = -(-NF * CB // RB)
LAG = 2
RELAY_LAG = 1
LEAD_TURN = CB
CHUNK = B // 2
NC = RB * B // CHUNK
F32 = jnp.float32
BF16 = jnp.bfloat16
MESH = pl.DeviceIdType.MESH
HBM = pl.BlockSpec(memory_space=pl.ANY)
SMEM = pl.BlockSpec(memory_space=pltpu.SMEM)
VMEM = pl.BlockSpec(memory_space=pltpu.VMEM)


def exchange(
    child, maptile, front, pattern,
    arrived_out, code, rows_out, match_out, pivots_out,
    child_v, arrived, front_v, rows, match, work, inv, pivots, map_v, code_v, code_s,
    a_send, a_recv, m_send, m_recv, x_send, x_recv, l_send, l_recv, t_send, t_recv,
    q_recv, qz_send, qy_send, qa_send, local,
):
    d = lax.axis_index("leaf")
    f = lax.axis_index("front")
    z, y = d // NY, d % NY
    x, core = f // 2, f % 2

    child_in = pltpu.make_async_copy(child, child_v, local.at[4])
    child_in.start()
    front_in = pltpu.make_async_copy(front.at[:, pl.ds(0, W)], front_v, local.at[3])

    @pl.when(f == 0)
    def _():
        front_in.start()

    barrier = pltpu.get_barrier_semaphore()

    def greet_leaf(k, _):
        pl.semaphore_signal(
            barrier, inc=1, device_id=(lax.rem(d + k, NL), f), device_id_type=MESH
        )
        return 0

    def greet_front(k, _):
        pl.semaphore_signal(
            barrier, inc=1, device_id=(d, lax.rem(f + k, NF)), device_id_type=MESH
        )
        return 0

    lax.fori_loop(1, NL, greet_leaf, 0)
    lax.fori_loop(1, NF, greet_front, 0)
    pl.semaphore_wait(barrier, NL - 1 + NF - 1)

    child_in.wait()

    def block_copy(to):
        return pltpu.make_async_remote_copy(
            src_ref=child_v.at[to], dst_ref=arrived.at[d], send_sem=a_send.at[to],
            recv_sem=a_recv.at[d], device_id=(to, f), device_id_type=MESH,
        )

    def map_copy(to):
        return pltpu.make_async_remote_copy(
            src_ref=maptile.at[to], dst_ref=map_v.at[d], send_sem=m_send.at[to],
            recv_sem=m_recv.at[d], device_id=(to, f), device_id_type=MESH,
        )

    def block_in(frm):
        return pltpu.make_async_remote_copy(
            src_ref=child_v.at[frm], dst_ref=arrived.at[frm], send_sem=a_send.at[frm],
            recv_sem=a_recv.at[frm], device_id=(frm, f), device_id_type=MESH,
        )

    def map_in(frm):
        return pltpu.make_async_remote_copy(
            src_ref=maptile.at[frm], dst_ref=map_v.at[frm], send_sem=m_send.at[frm],
            recv_sem=m_recv.at[frm], device_id=(frm, f), device_id_type=MESH,
        )

    own_block = pltpu.make_async_copy(child_v.at[d], arrived.at[d], local.at[0])
    own_map = pltpu.make_async_copy(maptile.at[d], map_v.at[d], local.at[1])

    def send_blocks():
        def step(k, _):
            early = jnp.where(k < NS, lax.rem(d + k, NS), NS + lax.rem(d + k, NL - NS))
            to = jnp.where(f == 0, early, lax.rem(d + k, NL))

            @pl.when(to != d)
            def _():
                map_copy(to).start()
                block_copy(to).start()

            return 0

        lax.fori_loop(0, NL, step, 0)

    def receive_blocks():
        def step(k, _):
            frm = lax.rem(d + k, NL)
            map_in(frm).wait_recv()
            block_in(frm).wait_recv()
            return 0

        lax.fori_loop(1, NL, step, 0)
        own_block.wait()
        own_map.wait()
        lane = lax.broadcasted_iota(jnp.int32, (8, B), 1)

        def latest(s, total):
            return jnp.maximum(total, jnp.where(map_v[s] == lane, s + 1, 0))

        code_v[...] = lax.fori_loop(0, NL, latest, jnp.zeros((8, B), jnp.int32))
        pltpu.make_async_copy(code_v, code, local.at[2]).start()
        pltpu.make_async_copy(arrived, arrived_out, local.at[0]).start()

    own_block.start()
    own_map.start()

    @pl.when(f != 1)
    def _():
        send_blocks()

    def chunk_of(j):
        return rows.at[pl.ds(pl.multiple_of(j * CHUNK, CHUNK), CHUNK)]

    def chunk_copy(j, to, way):
        return pltpu.make_async_remote_copy(
            src_ref=chunk_of(j), dst_ref=chunk_of(j), send_sem=x_send.at[j, way],
            recv_sem=x_recv.at[j], device_id=(d, to), device_id_type=MESH,
        )

    def root_next(j):
        return jnp.where(j % 2 == 0, 2, NF - 1)

    @pl.when(f == 0)
    def _():
        receive_blocks()
        to_smem = pltpu.make_async_copy(code_v, code_s, local.at[3])
        front_in.wait()
        to_smem.start()
        to_smem.wait()

        def form(r, _):
            r_glob = d * RB + r
            at = pl.ds(pl.multiple_of(r * B, B), B)
            for c in range(PANELS):
                t = code_s[0, r * CB + c]
                block = arrived[jnp.maximum(t - 1, 0)]
                has = (t > 0).astype(F32)
                keep = ((pattern[r, c] == 1) | (r_glob == c)) & (r_glob >= c)
                raw = front_v[at, c * B : (c + 1) * B]
                rows[at, c * B : (c + 1) * B] = (raw + block * has) * keep.astype(F32)
            for h in range(2):
                j = 2 * r + h
                chunk_copy(j, root_next(j), 0).start()
                chunk_copy(j, 1, 1).start()
            return 0

        lax.fori_loop(0, RB, form, 0)

    pair = f + 1 - 2 * core
    onward = f + 2 - 4 * core
    has_onward = ((core == 0) & (x < 3)) | ((core == 1) & (x > 1))

    def pass_on(n):
        j = 2 * n + core
        chunk_copy(j, 0, 0).wait_recv()

        @pl.when(f >= 2)
        def _():
            @pl.when(has_onward)
            def _():
                chunk_copy(j, onward, 0).start()

            chunk_copy(j, pair, 1).start()

        @pl.when((f == 1) & (n == 0))
        def _():
            send_blocks()

    def take_rest():
        def ending(n, _):
            chunk_copy(2 * n + 1 - core, 0, 0).wait_recv()
            return 0

        lax.fori_loop(0, NC // 2, ending, 0)

    def where_from(i, lead):
        r = 0 if lead else f * CB + i
        source = r // RB
        zs, ys = source // NY, source % NY
        return r % RB, ys, lax.rem(z - zs + NZ, NZ)

    def row_of(ref, i):
        return ref.at[pl.ds(pl.multiple_of(i * B, B), B)]

    def piece_of(ref, i, q):
        return ref.at[pl.ds(pl.multiple_of(i * B + q * PIECE, PIECE), PIECE)]

    def piece_copy(src, i, q, to_z, to_y, sem):
        return pltpu.make_async_remote_copy(
            src_ref=src, dst_ref=piece_of(match, i, q), send_sem=sem,
            recv_sem=q_recv.at[i, q], device_id=(to_z * NY + to_y, f), device_id_type=MESH,
        )

    def z_copy(src, i, up):
        to = lax.rem(z + (1 if up else NZ - 1), NZ)
        return piece_copy(src, i, y, to, y, qz_send.at[i, 0 if up else 1])

    def match_row(i, act, lead):
        r_loc, ys, zr = where_from(i, lead)
        held, r_at = (match, i) if lead else (rows, r_loc)
        at_source = (zr == 0) & (y == ys)

        @pl.when(at_source)
        def _():
            mine = piece_of(held, r_at, y)
            for k in range(1, NY):
                q = lax.rem(y + k, NY)
                act(piece_copy(piece_of(held, r_at, q), i, q, z, q, qa_send.at[i, k]))
            act(z_copy(mine, i, True))
            act(z_copy(mine, i, False))
            for k in (1, NY - 1):
                q = lax.rem(y + k, NY)
                act(piece_copy(mine, i, y, z, q, qy_send.at[i, k]))
            if not lead:
                act(
                    pltpu.make_async_copy(row_of(rows, r_loc), row_of(match, i), local.at[16 + i]),
                    here=True,
                )

        @pl.when(jnp.logical_not(at_source))
        def _():
            mine = piece_of(match, i, y)
            act(None, i, y)

            @pl.when(zr < NZ // 2)
            def _():
                act(z_copy(mine, i, True))

            @pl.when((zr == 0) | (zr > NZ // 2 + 1))
            def _():
                act(z_copy(mine, i, False))

            for k in (1, NY - 1):
                q = lax.rem(y + k, NY)

                @pl.when((zr != 0) | (q != ys))
                def _():
                    act(piece_copy(mine, i, y, z, q, qy_send.at[i, k]))

    def relay_row(i, act, lead):
        r_loc, ys, zr = where_from(i, lead)
        held, r_at = (match, i) if lead else (rows, r_loc)
        at_source = (zr == 0) & (y == ys)
        back = jnp.where(i % 2 == 0, NY - 1, 1)
        q, to = lax.rem(y + back, NY), lax.rem(y + NY - back, NY)

        @pl.when(at_source)
        def _():
            act(piece_copy(piece_of(held, r_at, q), i, q, z, to, qy_send.at[i, 0]))

        @pl.when(jnp.logical_not(at_source))
        def _():
            act(None, i, q)

            @pl.when((zr != 0) | (to != ys))
            def _():
                act(piece_copy(piece_of(match, i, q), i, q, z, to, qy_send.at[i, 0]))

            act(None, i, to, late=True)
            act(None, i, lax.rem(y + 2, NY), late=True)

    def piece_in(i, q):
        piece_copy(piece_of(match, i, q), i, q, z, lax.rem(y + 1, NY), qy_send.at[i, 1]).wait_recv()

    def begin(copy, i=None, q=None, late=False, here=False):
        if copy is not None:
            copy.start()
        elif not late:
            piece_in(i, q)

    def finish(copy, i=None, q=None, late=False, here=False):
        if copy is None:
            if late:
                piece_in(i, q)
        elif here:
            copy.wait()
        else:
            copy.wait_send()

    def run(turn, act, first, last, lead):
        def step(i, _):
            turn(i, act, lead)
            return 0

        lax.fori_loop(first, last, step, 0)

    def lead_copy(i, to, way):
        return pltpu.make_async_remote_copy(
            src_ref=row_of(match, i), dst_ref=row_of(match, i), send_sem=l_send.at[i - CB, way],
            recv_sem=l_recv.at[i - CB], device_id=(d, to), device_id_type=MESH,
        )

    def twin_copy(i, to):
        return pltpu.make_async_remote_copy(
            src_ref=row_of(match, i), dst_ref=row_of(match, i), send_sem=t_send.at[i - CB],
            recv_sem=t_recv.at[i - CB], device_id=(d, to), device_id_type=MESH,
        )

    is_root = (d == 0) & (f == 0)
    keep_pivots = pltpu.make_async_copy(pivots, pivots_out, local.at[6])

    def lead_done(k):
        match[pl.ds(pl.multiple_of((CB + k) * B, B), B), :] = inv[pl.ds(pl.multiple_of(k * B, B), B), :]
        lead_copy(CB + k, 2, 0).start()
        lead_copy(CB + k, NF - 2, 1).start()
        match_row(CB + k, begin, True)
        relay_row(CB + k, begin, True)

    def pass_lead(i):
        @pl.when((d == 0) & (f != 0))
        def _():
            lead_copy(i, 0, 0).wait_recv()

            @pl.when(f == 2)
            def _():
                lead_copy(i, 4, 0).start()

        match_row(i, begin, True)

    behind = jnp.where(f == 0, 0, jnp.where(d < NS, NC // 2, LAG))

    def turn(n, _):
        @pl.when((f != 0) & (n < NC // 2))
        def _():
            pass_on(n)

        @pl.when((f != 0) & (d < NS) & (n == NC // 2))
        def _():
            take_rest()

        m = n - behind

        @pl.when((m >= 0) & (m < CB))
        def _():
            match_row(m, begin, False)

        @pl.when((m >= RELAY_LAG) & (m < CB + RELAY_LAG))
        def _():
            relay_row(m - RELAY_LAG, begin, False)

        late = jnp.where(d == 0, 0, LEAD_TURN)
        i = m - jnp.where((f >= 5) & (d < NY), -LR, late) + CB
        takes_lead = (core == 0) & jnp.logical_not(is_root)

        @pl.when(takes_lead & (i >= CB) & (i < NR))
        def _():
            pass_lead(i)

        @pl.when(takes_lead & (i >= CB + RELAY_LAG) & (i < NR + RELAY_LAG))
        def _():
            relay_row(i - RELAY_LAG, begin, True)

        return 0

    lax.fori_loop(0, NC // 2 + max(CB, LEAD_TURN + LR) + RELAY_LAG, turn, 0)

    @pl.when(is_root)
    def _():
        work[...] = rows[0:W, :]
        factor_lead(work, pivots, inv, lead_done)
        keep_pivots.start()

    @pl.when((f != 0) & (d >= NS))
    def _():
        take_rest()

    keep_rows = pltpu.make_async_copy(rows, rows_out, local.at[7])
    keep_rows.start()

    @pl.when(f != 0)
    def _():
        receive_blocks()

    run(match_row, finish, 0, CB, False)
    run(relay_row, finish, 0, CB, False)
    keep_match = pltpu.make_async_copy(
        match.at[pl.ds(0, CB * B)], match_out.at[pl.ds(0, CB * B)], local.at[5]
    )
    keep_match.start()

    @pl.when(core == 0)
    def _():
        def hand_over(i, _):
            match_row(i, finish, True)
            relay_row(i, finish, True)
            twin_copy(i, f + 1).start()
            return 0

        lax.fori_loop(CB, NR, hand_over, 0)
        for i in range(CB, NR):
            twin_copy(i, f + 1).wait_send()

    @pl.when(core == 1)
    def _():
        for i in range(CB, NR):
            twin_copy(i, f - 1).wait_recv()

    keep_lead = pltpu.make_async_copy(
        match.at[pl.ds(CB * B, LR * B)], match_out.at[pl.ds(CB * B, LR * B)], local.at[8]
    )
    keep_lead.start()

    @pl.when(is_root)
    def _():
        for i in range(CB, NR):
            lead_copy(i, 2, 0).wait_send()
            lead_copy(i, NF - 2, 1).wait_send()
        keep_pivots.wait()

    @pl.when((d == 0) & (f == 2))
    def _():
        for i in range(CB, NR):
            lead_copy(i, 4, 0).wait_send()

    def sent(k, _):
        to = lax.rem(d + k, NL)
        map_copy(to).wait_send()
        block_copy(to).wait_send()
        return 0

    lax.fori_loop(1, NL, sent, 0)

    @pl.when(f == 0)
    def _():
        def chunk_sent(j, _):
            chunk_copy(j, root_next(j), 0).wait_send()
            chunk_copy(j, 1, 1).wait_send()
            return 0

        lax.fori_loop(0, NC, chunk_sent, 0)

    @pl.when(f >= 2)
    def _():
        def chunk_sent(n, _):
            j = 2 * n + core

            @pl.when(has_onward)
            def _():
                chunk_copy(j, onward, 0).wait_send()

            chunk_copy(j, pair, 1).wait_send()
            return 0

        lax.fori_loop(0, NC // 2, chunk_sent, 0)

    keep_rows.wait()
    keep_match.wait()
    keep_lead.wait()
    pltpu.make_async_copy(code_v, code, local.at[2]).wait()
    pltpu.make_async_copy(arrived, arrived_out, local.at[0]).wait()


def exchange_call(child, maptile, front, pattern):
    dma = pltpu.SemaphoreType.DMA
    shape = jax.ShapeDtypeStruct
    return pl.pallas_call(
        exchange,
        out_shape=(
            shape((NL, B, B), F32), shape((8, B), jnp.int32),
            shape((RB * B, W), F32), shape((NR * B, W), F32), shape((PANELS, B, B), F32),
        ),
        in_specs=[HBM, HBM, HBM, SMEM],
        out_specs=(HBM,) * 5,
        scratch_shapes=[
            pltpu.VMEM((NL, B, B), F32), pltpu.VMEM((NL, B, B), F32),
            pltpu.VMEM((RB * B, W), F32), pltpu.VMEM((RB * B, W), F32),
            pltpu.VMEM((NR * B, W), F32), pltpu.VMEM((W, W), F32), pltpu.VMEM((W, W), F32),
            pltpu.VMEM((PANELS, B, B), F32), pltpu.VMEM((NL, 8, B), jnp.int32),
            pltpu.VMEM((8, B), jnp.int32), pltpu.SMEM((8, B), jnp.int32),
            dma((NL,)), dma((NL,)), dma((NL,)), dma((NL,)), dma((NC, 2)), dma((NC,)),
            dma((LR, 2)), dma((LR,)), dma((LR,)), dma((LR,)),
            dma((NR, NY)), dma((NR, 2)), dma((NR, NY)), dma((NR, NY)), dma((16 + NR,)),
        ],
        compiler_params=pltpu.CompilerParams(
            collective_id=0, has_side_effects=True, vmem_limit_bytes=56 << 20
        ),
    )(child, maptile, front, pattern)


def factor_block(s):
    sub = lax.broadcasted_iota(jnp.int32, (8, B), 0)
    lane = lax.broadcasted_iota(jnp.int32, (8, B), 1)
    groups = B // 8

    def down(value, i):
        return jnp.broadcast_to(value[i : i + 1, :], (8, B))

    left = [s[8 * g : 8 * g + 8, :] for g in range(groups)]
    right = [(lane == sub + 8 * g).astype(F32) for g in range(groups)]
    upper, inverse = [], []
    for p in range(groups):
        cols = [
            [jnp.broadcast_to(left[g][:, 8 * p + i : 8 * p + i + 1], (8, B)) for g in range(p, groups)]
            for i in range(8)
        ]
        done_l = jnp.zeros((8, B), F32)
        done_r = jnp.zeros((8, B), F32)
        for i in range(8):
            scale = lax.rsqrt(down(cols[i][0], i))
            col = [value * scale for value in cols[i]]
            row_l = down(left[p], i) * scale
            row_r = down(right[p], i) * scale
            done_l = jnp.where(sub == i, row_l, done_l)
            done_r = jnp.where(sub == i, row_r, done_r)
            for k in range(i + 1, 8):
                at = down(col[0], k)
                cols[k] = [v - w * at for v, w in zip(cols[k], col)]
            for g in range(p, groups):
                left[g] = left[g] - col[g - p] * row_l
                right[g] = right[g] - col[g - p] * row_r
        upper.append(jnp.where(lane >= sub + 8 * p, done_l, 0.0))
        inverse.append(done_r)
    return jnp.concatenate(upper, 0), jnp.concatenate(inverse, 0)


def dot_exact(a, b, contract):
    return lax.dot_general(
        a, b, (contract, ((), ())), precision=lax.Precision.HIGHEST, preferred_element_type=F32
    )


NT = ((1,), (1,))
NN = ((1,), (0,))


def factor_lead(work, pivots, inv, done):
    r = lax.broadcasted_iota(jnp.int32, (B, B), 0)
    c = lax.broadcasted_iota(jnp.int32, (B, B), 1)
    row_block = lax.broadcasted_iota(jnp.int32, (W, B), 0) // B
    col_block = lax.broadcasted_iota(jnp.int32, (B, W), 1) // B
    inv[...] = jnp.zeros_like(inv)

    def panel(k, _):
        at = pl.ds(pl.multiple_of(k * B, B), B)
        pivot = work[at, at]
        upper, inverse = factor_block(jnp.where(r >= c, pivot, pivot.T))
        pivots[k] = upper.T
        lower = jnp.where(row_block > k, dot_exact(work[:, at], inverse, NT), 0.0)
        before = jnp.where(col_block < k, work[at, :], 0.0)
        inv[at, :] = -dot_exact(inverse, dot_exact(before, inv[...], NN), NN)
        inv[at, at] = inverse
        done(k)
        work[...] = work[...] - dot_exact(lower, lower, NT)
        work[:, at] = lower
        return 0

    lax.fori_loop(0, PANELS, panel, 0)


def halves(a):
    high = a.astype(BF16)
    return high, (a - high.astype(F32)).astype(BF16)


def dot_split(a, b):
    (ah, al), (bh, bl) = a, b
    dot = functools.partial(
        lax.dot_general, dimension_numbers=(NT, ((), ())), preferred_element_type=F32
    )
    return dot(ah, bh) + (dot(al, bh) + dot(ah, bl))


def solve(a, inv_h, inv_l):
    high, low = halves(a)
    n = W // 2
    left = dot_split((high[:, :n], low[:, :n]), (inv_h[:n, :n], inv_l[:n, :n]))
    right = dot_split((high, low), (inv_h[n:, :], inv_l[n:, :]))
    return jnp.concatenate([left, right], axis=1)


STEP = 2


def finish_kernel(
    code, pattern, front, rows, match, pivots, arrived, out,
    inv_h, inv_l, across_h, across_l,
):
    n = pl.program_id(0)
    d = lax.axis_index("leaf")
    f = lax.axis_index("front")

    @pl.when(n == 0)
    def _():
        inv_h[...], inv_l[...] = halves(match[CB * B :, :])
        for i in range(0, CB, STEP):
            at = slice(i * B, (i + STEP) * B)
            lower = solve(match[at, :], inv_h, inv_l)
            across_h[at, :], across_l[at, :] = halves(lower)

    lower = solve(rows[...], inv_h, inv_l)
    product = dot_split(halves(lower), (across_h[...], across_l[...]))
    for rr in range(STEP):
        r = n * STEP + rr
        r_glob = d * RB + r
        rs = slice(rr * B, rr * B + B)
        for c in range(CB):
            c_glob = f * CB + c
            cs = slice(c * B, c * B + B)
            t = code[0, r * CB + c]
            keep = ((pattern[r, c] == 1) | (r_glob == c_glob)) & (r_glob >= c_glob)
            active = (r_glob >= c_glob) & (c_glob >= PANELS)
            block = arrived[jnp.maximum(t - 1, 0)]
            value = (front[rs, cs] + block * (t > 0).astype(F32)) * keep.astype(F32)
            out[rs, cs] = value - product[rs, cs] * active.astype(F32)

        @pl.when(f == 0)
        def _():
            for c in range(PANELS):
                cs = slice(c * B, c * B + B)
                out[rs, cs] = lower[rs, cs] * (r_glob > c).astype(F32)

                @pl.when(r_glob == c)
                def _():
                    out[rs, cs] = pivots[c]


def finish_call(code, pattern, front, rows, match, pivots, arrived):
    whole = lambda *shape: pl.BlockSpec(shape, lambda n, *_: (0,) * len(shape))
    return pl.pallas_call(
        finish_kernel,
        out_shape=jax.ShapeDtypeStruct(front.shape, F32),
        grid_spec=pltpu.PrefetchScalarGridSpec(
            num_scalar_prefetch=2,
            grid=(RB // STEP,),
            in_specs=[
                pl.BlockSpec((STEP * B, CB * B), lambda n, *_: (n, 0)),
                pl.BlockSpec((STEP * B, W), lambda n, *_: (n, 0)),
                whole(NR * B, W),
                whole(PANELS, B, B),
                whole(NL, B, B),
            ],
            out_specs=pl.BlockSpec((STEP * B, CB * B), lambda n, *_: (n, 0)),
            scratch_shapes=[
                pltpu.VMEM((W, W), BF16), pltpu.VMEM((W, W), BF16),
                pltpu.VMEM((CB * B, W), BF16), pltpu.VMEM((CB * B, W), BF16),
            ],
        ),
        compiler_params=pltpu.CompilerParams(vmem_limit_bytes=56 << 20),
    )(code, pattern, front, rows, match, pivots, arrived)


def body(front, child_blocks, child_map, pattern):
    child = child_blocks.reshape(NL, B, B)
    maptile = jnp.broadcast_to(child_map.reshape(NL, 1, 1), (NL, 8, B))
    arrived, code, rows, match, pivots = exchange_call(child, maptile, front, pattern)
    return finish_call(code, pattern, front, rows, match, pivots, arrived)


def solution(mesh):
    placed = (
        P("leaf", "front"),
        P("leaf", None, None, "front"),
        P("leaf", None, "front"),
        P("leaf", "front"),
    )
    return jax.shard_map(
        body, mesh=mesh, in_specs=placed, out_specs=P("leaf", "front"), check_vma=False
    )
```
